256 devices in a mesh: rows: 16 (over x, z_lo), cols: 16 (over z_hi, y, core).
Axes of the slice: x: 4, y: 4, z: 8 (z_hi: 2, z_lo: 4; z = z_hi * 4 + z_lo), core: 2. Of those that a mesh axis runs over, the one named last changes fastest.
Arguments:
- matrix: bfloat16 [16384, 65536], P('rows', 'cols'), may hold values from -0.0234375 to 0.0234375
- cost_pred: bfloat16 [64, 65536], P(None, 'cols'), may hold values from -800 to 800
- cost_true: bfloat16 [64, 65536], P(None, 'cols'), may hold values from -1200 to 1200
- dual_start: float32 [64, 16384], P(None, 'rows'), may hold values from -3 to 3
- right_side: float32 [16384], P('rows'), may hold values from -3 to 3
- bound_code: int32 [65536], P('cols'), may hold values from 0 to 3
- step_numer: int32 [64, 3], replicated, may hold values from 2 to 9
- step_denom: int32 [64, 3], replicated, may hold values from 10 to 17
Outputs:
- primal_end: float32 [64, 65536], P(None, 'cols')
- dual_end: float32 [64, 16384], P(None, 'rows')
- cost_grad: float32 [64, 65536], P(None, 'cols')
The draws below stay inside these ranges and needn't reach their ends.
All inputs are finite; a program needn't handle non-finite values.
Results may differ from the reference program's by a relative error of at most 0.0017.
Values may be sent and summed in bfloat16 or wider, within the bound.
A program may use at most 64 MiB of HBM per device.

```python
import math
import jax
import jax.numpy as jnp
from jax import lax

VARS = 65536
INSTANCES = 64
ITERS = 2
ROWS = 16384


def cost_shape(key):
    keys = jax.random.split(key, 3)
    row_scale = jnp.exp(jax.random.uniform(keys[0], (INSTANCES, 1), jnp.float32, 0.0, math.log(10.0)))
    column_place = jnp.arange(VARS, dtype=jnp.float32)[None, :] / VARS
    column_rough = jax.random.uniform(keys[1], (1, VARS), jnp.float32, math.log(0.5), math.log(2.0))
    column_scale = jnp.exp(column_place * math.log(10.0) + column_rough)
    gauss = jnp.clip(jax.random.normal(keys[2], (INSTANCES, VARS), jnp.float32), -4.0, 4.0)
    spread = row_scale * column_scale
    return (gauss * spread, spread)


def draw_cost_pred(key, part):
    values, spread = cost_shape(key)
    return values.astype(jnp.bfloat16)


def draw_cost_true(key, part):
    values, spread = cost_shape(key)
    key = jax.random.fold_in(key, 7)
    noise = jnp.clip(jax.random.normal(key, (INSTANCES, VARS), jnp.float32), -4.0, 4.0)
    return (values + 0.5 * noise * spread).astype(jnp.bfloat16)


def set_ends(values, stream_key, least, largest):
    longest = values.shape.index(max(values.shape))
    spots = []
    for shift in (0, 1):
        where = [jax.random.randint(jax.random.fold_in(stream_key, axis), (), 0, length) for axis, length in enumerate(values.shape)]
        where[longest] = (where[longest] + shift) % values.shape[longest]
        spots.append(tuple(where))
    return values.at[spots[0]].set(least).at[spots[1]].set(largest)


def shard_levels(own_key, dims, pieces, smallest, top_value):
    gain, own = 1.0, jax.random.fold_in(own_key, 6)
    for position, blocks in pieces:
        steps = jnp.exp(jax.random.uniform(jax.random.fold_in(own, position), (blocks,), jnp.float32, smallest / len(pieces), top_value / len(pieces)))
        gain = gain * jnp.repeat(steps, dims[position] // blocks).reshape([-1 if axis == position else 1 for axis in range(len(dims))])
    return gain


def bell_draw(key, extent, scale, limit, cuts=(), kind=jnp.bfloat16):
    factor_of = shard_levels(key, extent, cuts, -0.22, 0.18) if cuts else 1.0
    array = jax.random.normal(key, extent, jnp.float32) * scale * factor_of
    return jnp.minimum(jnp.maximum(array, -limit), limit).astype(kind)


def setup_inputs(seed: int = 0) -> dict:
    seeds = jax.random.split(jax.random.key(seed), 9)
    return {
        "matrix": bell_draw(seeds[0], (ROWS, VARS), VARS ** -0.5, 0.0234375, ((0, 16), (1, 16))),
        "cost_pred": draw_cost_pred(jax.random.fold_in(seeds[8], 71), 0),
        "cost_true": draw_cost_true(jax.random.fold_in(seeds[8], 71), 0),
        "dual_start": bell_draw(seeds[3], (INSTANCES, ROWS), 0.5, 3.0, ((1, 16),), jnp.float32),
        "right_side": bell_draw(seeds[4], (ROWS,), 0.5, 3.0, ((0, 16),), jnp.float32),
        "bound_code": set_ends(jax.random.randint(seeds[5], (VARS,), 0, 4), jax.random.fold_in(seeds[5], 1), 0, 3).astype(jnp.int32),
        "step_numer": set_ends(jax.random.randint(seeds[6], (INSTANCES, 3), 2, 10), jax.random.fold_in(seeds[6], 1), 2, 9).astype(jnp.int32),
        "step_denom": set_ends(jax.random.randint(seeds[7], (INSTANCES, 3), 10, 18), jax.random.fold_in(seeds[7], 1), 10, 17).astype(jnp.int32),
    }


sharpness = 16.0
eps_norm = 1e-06

def smooth_slope(shifted, lower_bound, upper_bound):
    return jax.nn.sigmoid(sharpness * (shifted - lower_bound)) * jax.nn.sigmoid(sharpness * (upper_bound - shifted))

def bounds_of(bound_code):
    low_bit = (bound_code % 2).astype(jnp.float32)
    high_bit = (bound_code // 2).astype(jnp.float32)
    return (-0.25 - 0.75 * low_bit, 0.25 + 0.75 * high_bit)

def times_matrix(dual_bf, matrix):
    return jnp.dot(dual_bf, matrix, preferred_element_type=jnp.float32)

def matrix_times(primal_bf, matrix):
    return lax.dot_general(primal_bf, matrix, (((1,), (1,)), ((), ())), preferred_element_type=jnp.float32)

def reference(matrix, cost_pred, cost_true, dual_start, right_side, bound_code, step_numer, step_denom):
    costs = cost_pred.astype(jnp.float32)
    ratios = step_numer.astype(jnp.float32) / step_denom.astype(jnp.float32)
    cost_scale = jnp.sqrt(lax.optimization_barrier(jnp.sum(costs * costs, axis=1, keepdims=True)) / VARS + eps_norm)
    tau_step = ratios[:, 0:1] / cost_scale
    sigma_step = ratios[:, 1:2] * cost_scale
    theta_step = ratios[:, 2:3]
    lower_bound, upper_bound = bounds_of(bound_code)
    primal = jnp.zeros_like(costs)
    dual_state = dual_start.astype(jnp.float32)
    history = []
    for turn in range(ITERS):
        reduced = costs - times_matrix(dual_state.astype(jnp.bfloat16), matrix)
        shifted = primal - tau_step * reduced
        projected = jnp.clip(shifted, lower_bound, upper_bound)
        extended = projected + theta_step * (projected - primal)
        residue = right_side[None, :] - matrix_times(extended.astype(jnp.bfloat16), matrix)
        dual_state = dual_state + sigma_step * residue
        history.append((reduced, shifted, residue))
        primal = projected
    adjoint_primal = cost_true.astype(jnp.float32)
    adjoint_dual = None
    factors = jnp.zeros_like(cost_scale)
    gradient = jnp.zeros_like(costs)
    for turn in reversed(range(ITERS)):
        reduced, shifted, residue = history[turn]
        carried = jnp.zeros_like(costs)
        forward_adj = adjoint_primal
        if adjoint_dual is not None:
            factors = factors + sigma_step * lax.optimization_barrier(jnp.sum(adjoint_dual * residue, axis=1, keepdims=True))
            backward_adj = -sigma_step * times_matrix(adjoint_dual.astype(jnp.bfloat16), matrix)
            forward_adj = adjoint_primal + (1.0 + theta_step) * backward_adj
            carried = -theta_step * backward_adj
        slope_adj = smooth_slope(shifted, lower_bound, upper_bound) * forward_adj
        factors = factors + tau_step * lax.optimization_barrier(jnp.sum(slope_adj * reduced, axis=1, keepdims=True))
        gradient = gradient - tau_step * slope_adj
        adjoint_primal = slope_adj + carried
        if turn > 0:
            pushed = matrix_times((tau_step * slope_adj).astype(jnp.bfloat16), matrix)
            adjoint_dual = pushed if adjoint_dual is None else adjoint_dual + pushed
    gradient = gradient + costs * factors / (VARS * cost_scale * cost_scale)
    return (primal, dual_state, gradient)
```

```python
import jax
import jax.numpy as jnp
from jax import lax
from jax.experimental import pallas as pl
from jax.experimental.pallas import tpu as pltpu
from jax.sharding import PartitionSpec as P

VARS = 65536
MESH = pl.DeviceIdType.MESH
F32 = jnp.float32
BF16 = jnp.bfloat16
SHARP = 16.0
EPS = 1e-06

INST = 64
HALF = 32
ROWS = 1024
COLS = 4096
SIDE = 4
WIDE = COLS // SIDE
CHUNK = WIDE // SIDE
TEAM = 8
PIECE = ROWS // TEAM
LANES = 128


def kernel(
    m_hbm, cp_ref, ct_ref, d0_ref, right_ref, code_ref, numer_ref, denom_ref,
    primal_ref, dual_ref, grad_ref,
    m_ref, m_sem,
    tau_ref, sigma_ref, theta_ref, scale2_ref, low_ref, high_ref, sum_ref,
    dbf_ref, own0_ref, own1_ref, t0_ref, t1_ref, red0_ref, sh0_ref, slope0_ref, sa1_ref, e_ref, z_ref,
    s1x, s1z, r1x, r1z, s2z, s2x, r2z, r2x, gather,
    a_ss, a_rs, f_ss, f_rs,
    sb, rb, zs, zr, gb, gd,
    b_ss, b_rs, z_ss, z_rs, g_ss, g_rs, gd_ss, gd_rs,
    rows_t, rows_p, rows_pr, rowx, rowz,
    t_ss, t_rs, p_ss, p_rs, rx_ss, rx_rs, rz_ss, rz_rs,
    dual1_ref, weigh_ref, wimg_ref,
):
    rr = lax.axis_index("rows")
    cc = lax.axis_index("cols")
    x, zl = rr // SIDE, lax.rem(rr, SIDE)
    zh, yc = cc // TEAM, lax.rem(cc, TEAM)
    y, core = yc // 2, lax.rem(yc, 2)

    def around(value, step, size):
        return lax.rem(value + step + size, size)

    def x_peer(k):
        return (around(x, k, SIDE) * SIDE + zl, cc)

    def z_peer(k):
        return (x * SIDE + around(zl, k, SIDE), cc)

    def team_peer(k):
        return (rr, zh * TEAM + around(yc, k, TEAM))

    far_peer = (rr, (1 - zh) * TEAM + yc)

    def remote(src, dst, send, recv, peer):
        copy = pltpu.make_async_remote_copy(
            src_ref=src, dst_ref=dst, send_sem=send, recv_sem=recv, device_id=peer, device_id_type=MESH
        )
        copy.start()
        return copy

    def at(value, size):
        return pl.ds(pl.multiple_of(value * size, size), size)

    order = (2, 1, 3, 0)
    loads = []
    for k in order:
        cols = at(around(x, k, SIDE), WIDE)
        load = pltpu.make_async_copy(m_hbm.at[:, cols], m_ref.at[:, cols], m_sem.at[k])
        load.start()
        loads.append(load)

    barrier = pltpu.get_barrier_semaphore()
    for k in (1, 2, 3):
        pl.semaphore_signal(barrier, inc=1, device_id=x_peer(k), device_id_type=MESH)
        pl.semaphore_signal(barrier, inc=1, device_id=z_peer(k), device_id_type=MESH)
    for k in range(1, TEAM):
        pl.semaphore_signal(barrier, inc=1, device_id=team_peer(k), device_id_type=MESH)
    pl.semaphore_signal(barrier, inc=1, device_id=far_peer, device_id_type=MESH)

    lane = lax.broadcasted_iota(jnp.int32, (INST, LANES), 1)
    diagonal = lane == lax.broadcasted_iota(jnp.int32, (INST, LANES), 0)

    def to_row(column):
        spread = jnp.where(diagonal, jnp.broadcast_to(column, (INST, LANES)), 0.0)
        return jnp.broadcast_to(jnp.sum(spread, axis=0, keepdims=True), (8, LANES))

    def to_column(row):
        spread = jnp.where(diagonal, jnp.broadcast_to(row[0:1, :], (INST, LANES)), 0.0)
        return jnp.sum(spread, axis=1, keepdims=True)

    sum_ref[...] = jnp.zeros_like(sum_ref)

    def square_step(i, _):
        c = cp_ref[:, at(i, LANES)].astype(F32)
        sum_ref[...] += c * c
        return 0

    lax.fori_loop(0, COLS // LANES, square_step, 0, unroll=4)
    squares = jnp.sum(sum_ref[...], axis=1, keepdims=True)
    rows_t[0, yc] = to_row(squares)

    dbf_ref[...] = d0_ref[...].astype(BF16)
    code = code_ref[...]
    half_code = code // 2
    low_ref[...] = -0.25 - 0.75 * (code - 2 * half_code).astype(F32)
    high_ref[...] = 0.25 + 0.75 * half_code.astype(F32)
    theta_ref[...] = jnp.broadcast_to(numer_ref[:, 2:3].astype(F32) / denom_ref[:, 2:3].astype(F32), (INST, LANES))

    pl.semaphore_wait(barrier, 14)

    def team_rows(which):
        return [
            remote(rows_t.at[which, yc], rows_t.at[which, yc], t_ss.at[which, k - 1], t_rs.at[which, k - 1], team_peer(k))
            for k in range(1, TEAM)
        ]

    def wait_all(copies):
        for c in copies:
            c.wait()

    def sum_team(which):
        total = rows_t[which, 0]
        for i in range(1, TEAM):
            total = total + rows_t[which, i]
        return total

    def far_row(which):
        return remote(rows_p.at[which], rows_pr.at[which], p_ss.at[which], p_rs.at[which], far_peer)

    norm_copies = team_rows(0)

    def scatter_dual(first):
        sends = []
        for position, k in enumerate(order):
            j = around(x, k, SIDE)
            if first:
                loads[position].wait()
            out = jnp.dot(dbf_ref[...], m_ref[:, at(j, WIDE)], preferred_element_type=F32)
            if k:
                s1x[k - 1] = out[:HALF].astype(BF16)
                sends.append(remote(s1x.at[k - 1], r1x.at[k - 1], a_ss.at[0, k - 1], a_rs.at[0, k - 1], x_peer(k)))
            else:
                own0_ref[...] = out[:HALF]
            own1_ref[j] = out[HALF:]
        for k in (2, 1, 3):
            cols = at(around(zl, k, SIDE), CHUNK)
            s1z[k - 1] = own1_ref[:, :, cols].astype(BF16)
            sends.append(remote(s1z.at[k - 1], r1z.at[k - 1], a_ss.at[1, k - 1], a_rs.at[1, k - 1], z_peer(k)))
        return sends

    def second_dual(sends):
        later = []
        for c in sends[:3]:
            c.wait()
        t0_ref[...] = own0_ref[...] + r1x[0].astype(F32) + r1x[1].astype(F32) + r1x[2].astype(F32)
        for k in (2, 1, 3):
            s2z[k - 1] = t0_ref[:, at(around(zl, k, SIDE), CHUNK)].astype(BF16)
            later.append(remote(s2z.at[k - 1], r2z.at[k - 1], a_ss.at[2, k - 1], a_rs.at[2, k - 1], z_peer(k)))
        for c in sends[3:]:
            c.wait()
        t1_ref[...] = own1_ref[:, :, at(zl, CHUNK)] + r1z[0].astype(F32) + r1z[1].astype(F32) + r1z[2].astype(F32)
        for k in (2, 1, 3):
            s2x[k - 1] = t1_ref[around(x, k, SIDE)].astype(BF16)
            later.append(remote(s2x.at[k - 1], r2x.at[k - 1], a_ss.at[3, k - 1], a_rs.at[3, k - 1], x_peer(k)))
        return later

    def gather_dual(later):
        wait_all(later)
        upper = t0_ref[:, at(zl, CHUNK)] + r2z[0].astype(F32) + r2z[1].astype(F32) + r2z[2].astype(F32)
        lower = t1_ref[x] + r2x[0].astype(F32) + r2x[1].astype(F32) + r2x[2].astype(F32)
        gather[x, zl, :HALF] = upper.astype(BF16)
        gather[x, zl, HALF:] = lower.astype(BF16)
        mine = gather.at[x, zl]
        z_own = {}
        x_own = {}
        for k in (1, 3, 2):
            z_own[k] = remote(mine, mine, a_ss.at[4, k - 1], a_rs.at[4, k - 1], z_peer(k))
            x_own[k] = remote(mine, mine, a_ss.at[5, k - 1], a_rs.at[5, k - 1], x_peer(k))
        forwards = []
        for k in (1, 3, 2):
            z_own[k].wait()
            part = gather.at[x, around(zl, -k, SIDE), pl.ds(0, HALF)]
            for q in (1, 3, 2):
                forwards.append(remote(part, part, f_ss.at[0, k - 1, q - 1], f_rs.at[0, k - 1, q - 1], x_peer(q)))
            x_own[k].wait()
            part = gather.at[around(x, -k, SIDE), zl, pl.ds(HALF, HALF)]
            for q in (1, 3, 2):
                forwards.append(remote(part, part, f_ss.at[1, k - 1, q - 1], f_rs.at[1, k - 1, q - 1], z_peer(q)))
        wait_all(forwards)

    def each_piece(body):
        def step(i, _):
            gx = i // (SIDE * 2)
            gz = lax.rem(i // 2, SIDE)
            part = lax.rem(i, 2)
            body(gx, gz, at(part, LANES), at(i, LANES))
            return 0

        lax.fori_loop(0, COLS // LANES, step, 0, unroll=2)

    def primal_images(use, lhs_rows, lhs_uses):
        sends = []
        for k in (2, 1, 3, 0):
            yk = around(y, k, SIDE)
            out = lax.dot_general(
                e_ref[lhs_rows, :], m_ref[at(yk, 2 * PIECE), :], (((1,), (1,)), ((), ())), preferred_element_type=F32
            )
            for n, u in enumerate(lhs_uses):
                z_ref[u, yk * 2] = out[n * INST : (n + 1) * INST, :PIECE]
                z_ref[u, yk * 2 + 1] = out[n * INST : (n + 1) * INST, PIECE:]

    def scatter_primal(u):
        sends = []
        for k in (4, 5, 3, 2, 6, 1, 7):
            sb[u, k - 1] = z_ref[u, around(yc, k, TEAM)].astype(BF16)
            sends.append(remote(sb.at[u, k - 1], rb.at[u, k - 1], b_ss.at[u, k - 1], b_rs.at[u, k - 1], team_peer(k)))
        return sends

    def far_primal(u, sends):
        wait_all(sends)
        total = z_ref[u, yc]
        for k in range(1, TEAM):
            total = total + rb[u, k - 1].astype(F32)
        zs[u] = total.astype(BF16)
        return remote(zs.at[u], zr.at[u], z_ss.at[u], z_rs.at[u], far_peer)

    def done_primal(u, copy):
        copy.wait()
        return zs[u].astype(F32) + zr[u].astype(F32)

    def gather_primal(v):
        return [
            remote(gb.at[v, yc], gb.at[v, yc], g_ss.at[v, k - 1], g_rs.at[v, k - 1], team_peer(k))
            for k in (4, 5, 3, 2, 6, 1, 7)
        ]

    def fill_dual(v):
        for i in range(TEAM):
            dbf_ref[:, i * PIECE : (i + 1) * PIECE] = gb[v, i]

    own_cols = at(yc, PIECE)

    sends = scatter_dual(True)
    wait_all(norm_copies)
    rows_p[0] = sum_team(0)
    norm_far = far_row(0)
    later = second_dual(sends)
    norm_far.wait()
    norm_sum = to_column(rows_p[0] + rows_pr[0])
    scale = jnp.sqrt(norm_sum / VARS + EPS)
    tau_ref[...] = jnp.broadcast_to(numer_ref[:, 0:1].astype(F32) / denom_ref[:, 0:1].astype(F32) / scale, (INST, LANES))
    sigma_ref[...] = jnp.broadcast_to(numer_ref[:, 1:2].astype(F32) / denom_ref[:, 1:2].astype(F32) * scale, (INST, LANES))
    scale2_ref[...] = jnp.broadcast_to(VARS * scale * scale, (INST, LANES))
    gather_dual(later)

    def first_step(gx, gz, lanes, cols):
        image = gather[gx, gz, :, lanes].astype(F32)
        reduced = cp_ref[:, cols].astype(F32) - image
        shifted = 0.0 - tau_ref[...] * reduced
        projected = jnp.minimum(jnp.maximum(shifted, low_ref[:, cols]), high_ref[:, cols])
        red0_ref[:, cols] = reduced
        sh0_ref[:, cols] = shifted
        e_ref[:INST, cols] = (projected + theta_ref[...] * projected).astype(BF16)

    each_piece(first_step)

    primal_images(0, slice(0, INST), (0,))
    sends = scatter_primal(0)

    def slope_of(shifted, cols):
        return jax.nn.sigmoid(SHARP * (shifted - low_ref[:, cols])) * jax.nn.sigmoid(
            SHARP * (high_ref[:, cols] - shifted)
        )

    def slope_step(gx, gz, lanes, cols):
        slope = slope_of(sh0_ref[:, cols], cols)
        slope0_ref[:, cols] = slope
        e_ref[INST:, cols] = (slope * red0_ref[:, cols]).astype(BF16)

    each_piece(slope_step)
    primal_images(1, slice(INST, 2 * INST), (1,))
    far = far_primal(0, sends)
    weigh_sends = scatter_primal(1)
    image = done_primal(0, far)
    residue0 = right_ref[:, own_cols] - image
    dual1 = d0_ref[:, own_cols] + sigma_ref[...] * residue0
    dual1_ref[...] = dual1
    weigh_ref[...] = sigma_ref[...] * residue0
    gb[0, yc] = dual1.astype(BF16)
    wait_all(gather_primal(0))
    fill_dual(0)

    sends = scatter_dual(False)
    weigh_far = far_primal(1, weigh_sends)
    later = second_dual(sends)
    wimg_ref[...] = (
        tau_ref[...] * (1.0 + theta_ref[...]) * sigma_ref[...] * done_primal(1, weigh_far)
    )
    gather_dual(later)
    sum_ref[...] = jnp.zeros_like(sum_ref)

    def second_step(gx, gz, lanes, cols):
        image = gather[gx, gz, :, lanes].astype(F32)
        low, high = low_ref[:, cols], high_ref[:, cols]
        reduced = cp_ref[:, cols].astype(F32) - image
        before = jnp.minimum(jnp.maximum(sh0_ref[:, cols], low), high)
        shifted = before - tau_ref[...] * reduced
        projected = jnp.minimum(jnp.maximum(shifted, low), high)
        primal_ref[:, cols] = projected
        e_ref[INST:, cols] = (projected + theta_ref[...] * (projected - before)).astype(BF16)
        slope_adj = slope_of(shifted, cols) * ct_ref[:, cols].astype(F32)
        sa1_ref[:, cols] = slope_adj
        e_ref[:INST, cols] = (tau_ref[...] * slope_adj).astype(BF16)
        sum_ref[...] += slope_adj * reduced + slope_adj * (slope0_ref[:, cols] * red0_ref[:, cols])

    each_piece(second_step)
    rows_t[1, yc] = to_row(tau_ref[:, 0:1] * jnp.sum(sum_ref[...], axis=1, keepdims=True))

    primal_images(2, slice(0, 2 * INST), (2, 3))
    sends = scatter_primal(2)
    factor_copies = team_rows(1)
    far = far_primal(2, sends)
    end_sends = scatter_primal(3)
    wait_all(factor_copies)
    rows_p[1] = sum_team(1)
    factor_far = far_row(1)
    adjoint = done_primal(2, far)
    rounded = adjoint.astype(BF16)
    gb[1, yc] = rounded
    gathers = gather_primal(1)
    weighed = adjoint * weigh_ref[...] - rounded.astype(F32) * wimg_ref[...]
    rows_t[2, yc] = to_row(jnp.sum(weighed, axis=1, keepdims=True))
    factor_copies = team_rows(2)
    wait_all(gathers)
    fill_dual(1)

    sends = scatter_dual(False)
    end_far = far_primal(3, end_sends)
    wait_all(factor_copies)
    rowx[x] = sum_team(2)
    x_rows = [remote(rowx.at[x], rowx.at[x], rx_ss.at[k - 1], rx_rs.at[k - 1], x_peer(k)) for k in (1, 2, 3)]
    later = second_dual(sends)
    wait_all(x_rows)
    rowz[zl] = rowx[0] + rowx[1] + rowx[2] + rowx[3]
    z_rows = [remote(rowz.at[zl], rowz.at[zl], rz_ss.at[k - 1], rz_rs.at[k - 1], z_peer(k)) for k in (1, 2, 3)]
    factor_far.wait()
    residue1 = right_ref[:, own_cols] - done_primal(3, end_far)
    gd[yc] = dual1_ref[...] + sigma_ref[...] * residue1
    dual_gathers = [
        remote(gd.at[yc], gd.at[yc], gd_ss.at[k - 1], gd_rs.at[k - 1], team_peer(k)) for k in (4, 5, 3, 2, 6, 1, 7)
    ]
    gather_dual(later)
    wait_all(z_rows)
    factors = to_column(rows_p[1] + rows_pr[1] + (rowz[0] + rowz[1] + rowz[2] + rowz[3]))
    sum_ref[...] = jnp.broadcast_to(factors, (INST, LANES)) / scale2_ref[...]

    def last_step(gx, gz, lanes, cols):
        image = gather[gx, gz, :, lanes].astype(F32)
        slope_adj = sa1_ref[:, cols]
        ahead = slope_adj - (1.0 + theta_ref[...]) * (sigma_ref[...] * image)
        gradient = tau_ref[...] * (slope_adj + slope0_ref[:, cols] * ahead)
        grad_ref[:, cols] = cp_ref[:, cols].astype(F32) * sum_ref[...] - gradient

    each_piece(last_step)
    wait_all(dual_gathers)
    for i in range(TEAM):
        dual_ref[:, i * PIECE : (i + 1) * PIECE] = gd[i]


def local(matrix, cost_pred, cost_true, dual_start, right_side, bound_code, step_numer, step_denom):
    dma = pltpu.SemaphoreType.DMA
    v = pltpu.VMEM
    whole = pl.BlockSpec(memory_space=pltpu.VMEM)
    uses, rows = 4, 3
    scratch = [
        v((ROWS, COLS), BF16), dma((SIDE,)),
        v((INST, LANES), F32), v((INST, LANES), F32), v((INST, LANES), F32), v((INST, LANES), F32),
        v((1, COLS), F32), v((1, COLS), F32), v((INST, LANES), F32),
        v((INST, ROWS), BF16), v((HALF, WIDE), F32), v((SIDE, HALF, WIDE), F32), v((HALF, WIDE), F32),
        v((SIDE, HALF, CHUNK), F32), v((INST, COLS), F32), v((INST, COLS), F32), v((INST, COLS), F32),
        v((INST, COLS), F32), v((2 * INST, COLS), BF16), v((uses, TEAM, INST, PIECE), F32),
        v((3, HALF, WIDE), BF16), v((3, SIDE, HALF, CHUNK), BF16), v((3, HALF, WIDE), BF16), v((3, SIDE, HALF, CHUNK), BF16),
        v((3, HALF, CHUNK), BF16), v((3, HALF, CHUNK), BF16), v((3, HALF, CHUNK), BF16), v((3, HALF, CHUNK), BF16),
        v((SIDE, SIDE, INST, CHUNK), BF16),
        dma((6, 3)), dma((6, 3)), dma((2, 3, 3)), dma((2, 3, 3)),
        v((uses, TEAM - 1, INST, PIECE), BF16), v((uses, TEAM - 1, INST, PIECE), BF16),
        v((uses, INST, PIECE), BF16), v((uses, INST, PIECE), BF16),
        v((2, TEAM, INST, PIECE), BF16), v((TEAM, INST, PIECE), F32),
        dma((uses, TEAM - 1)), dma((uses, TEAM - 1)), dma((uses,)), dma((uses,)),
        dma((2, TEAM - 1)), dma((2, TEAM - 1)), dma((TEAM - 1,)), dma((TEAM - 1,)),
        v((rows, TEAM, 8, LANES), F32), v((2, 8, LANES), F32), v((2, 8, LANES), F32), v((SIDE, 8, LANES), F32),
        v((SIDE, 8, LANES), F32),
        dma((rows, TEAM - 1)), dma((rows, TEAM - 1)), dma((2,)), dma((2,)), dma((3,)), dma((3,)), dma((3,)), dma((3,)),
        v((INST, PIECE), F32), v((INST, PIECE), F32), v((INST, PIECE), F32),
    ]
    return pl.pallas_call(
        kernel,
        out_shape=(
            jax.ShapeDtypeStruct((INST, COLS), F32),
            jax.ShapeDtypeStruct((INST, ROWS), F32),
            jax.ShapeDtypeStruct((INST, COLS), F32),
        ),
        in_specs=[pl.BlockSpec(memory_space=pl.ANY)] + [whole] * 7,
        out_specs=(whole, whole, whole),
        scratch_shapes=scratch,
        compiler_params=pltpu.CompilerParams(
            collective_id=0, has_side_effects=True, vmem_limit_bytes=52 * 2**20
        ),
    )(
        matrix,
        cost_pred,
        cost_true,
        dual_start,
        right_side.reshape(1, ROWS),
        bound_code.reshape(1, COLS),
        step_numer,
        step_denom,
    )


def solution(mesh):
    placed = (
        P("rows", "cols"),
        P(None, "cols"),
        P(None, "cols"),
        P(None, "rows"),
        P("rows"),
        P("cols"),
        P(),
        P(),
    )
    return jax.shard_map(
        local,
        mesh=mesh,
        in_specs=placed,
        out_specs=(P(None, "cols"), P(None, "rows"), P(None, "cols")),
        check_vma=False,
    )
```

```python
import jax
import jax.numpy as jnp
from jax import lax
from jax.experimental import pallas as pl
from jax.experimental.pallas import tpu as pltpu
from jax.sharding import PartitionSpec as P

VARS = 65536
MESH = pl.DeviceIdType.MESH
F32 = jnp.float32
BF16 = jnp.bfloat16
SHARP = 16.0
EPS = 1e-06

INST = 64
HALF = 32
ROWS = 1024
COLS = 4096
SIDE = 4
WIDE = COLS // SIDE
CHUNK = WIDE // SIDE
TEAM = 8
PIECE = ROWS // TEAM
LANES = 128


def kernel(
    m_hbm, cp_hbm, ct_hbm, d0_hbm, right_hbm, code_hbm, numer_hbm, denom_hbm,
    primal_out, dual_out, grad_out,
    primal_ref, dual_ref, grad_ref, out_sem, m_ref, m_sem, cp_ref, ct_ref, d0_ref, right_ref, code_ref, numer_ref, denom_ref, in_sem,
    tau_ref, sigma_ref, theta_ref, scale2_ref, low_ref, high_ref, sum_ref,
    dbf_ref, own0_ref, own1_ref, t0_ref, t1_ref, red0_ref, sh0_ref, slope0_ref, sa1_ref, e_ref, z_ref,
    s1x, s1z, r1x, r1z, s2z, s2x, r2z, r2x, gather,
    a_ss, a_rs, s_ss, s_rs, f_ss, f_rs,
    sb, rb, zs, zr, gb, gd,
    b_ss, b_rs, z_ss, z_rs, g_ss, g_rs, gd_ss, gd_rs,
    rows_t, rows_p, rows_pr, rowx, rowz,
    t_ss, t_rs, p_ss, p_rs, rx_ss, rx_rs, rz_ss, rz_rs,
    dual1_ref, weigh_ref, wimg_ref,
):
    rr = lax.axis_index("rows")
    cc = lax.axis_index("cols")
    x, zl = rr // SIDE, lax.rem(rr, SIDE)
    zh, yc = cc // TEAM, lax.rem(cc, TEAM)
    y = yc // 2

    def flip(value, k):
        if k == 0:
            return value
        total = value
        for bit in (1, 2, 4):
            if k & bit:
                total = total + bit - 2 * bit * lax.rem(value // bit, 2)
        return total

    def x_peer(k):
        return (flip(x, k) * SIDE + zl, cc)

    def z_peer(k):
        return (x * SIDE + flip(zl, k), cc)

    def team_peer(k):
        return (rr, zh * TEAM + flip(yc, k))

    far_peer = (rr, (1 - zh) * TEAM + yc)

    def remote(src, dst, send, recv, peer):
        copy = pltpu.make_async_remote_copy(
            src_ref=src, dst_ref=dst, send_sem=send, recv_sem=recv, device_id=peer, device_id_type=MESH
        )
        copy.start()
        return copy

    def at(value, size):
        return pl.ds(pl.multiple_of(value * size, size), size)

    order = (2, 1, 3, 0)
    near_last = (2, 3, 1)
    team_order = (4, 5, 6, 7, 2, 3, 1)

    def load(n, src, dst):
        copy = pltpu.make_async_copy(src, dst, in_sem.at[n])
        copy.start()
        return copy

    load_d0 = load(0, d0_hbm, d0_ref)
    load_cp = load(1, cp_hbm, cp_ref)
    m_loads = []
    for k in order:
        cols = at(flip(x, k), WIDE)
        copy = pltpu.make_async_copy(m_hbm.at[:, cols], m_ref.at[:, cols], m_sem.at[k])
        copy.start()
        m_loads.append(copy)
    small_loads = [
        load(2, right_hbm, right_ref), load(3, code_hbm, code_ref),
        load(4, numer_hbm, numer_ref), load(5, denom_hbm, denom_ref),
    ]
    load_ct = load(6, ct_hbm, ct_ref)

    barrier = pltpu.get_barrier_semaphore()
    for k in (1, 2, 3):
        pl.semaphore_signal(barrier, inc=1, device_id=x_peer(k), device_id_type=MESH)
        pl.semaphore_signal(barrier, inc=1, device_id=z_peer(k), device_id_type=MESH)
    for k in range(1, TEAM):
        pl.semaphore_signal(barrier, inc=1, device_id=team_peer(k), device_id_type=MESH)
    pl.semaphore_signal(barrier, inc=1, device_id=far_peer, device_id_type=MESH)

    lane = lax.broadcasted_iota(jnp.int32, (INST, LANES), 1)
    diagonal = lane == lax.broadcasted_iota(jnp.int32, (INST, LANES), 0)

    def to_row(column):
        spread = jnp.where(diagonal, jnp.broadcast_to(column, (INST, LANES)), 0.0)
        return jnp.broadcast_to(jnp.sum(spread, axis=0, keepdims=True), (8, LANES))

    def to_column(row):
        spread = jnp.where(diagonal, jnp.broadcast_to(row[0:1, :], (INST, LANES)), 0.0)
        return jnp.sum(spread, axis=1, keepdims=True)

    square = lax.broadcasted_iota(jnp.int32, (INST, INST), 1) == lax.broadcasted_iota(jnp.int32, (INST, INST), 0)

    def ratio(n):
        row = numer_ref[n : n + 1, :].astype(F32) / denom_ref[n : n + 1, :].astype(F32)
        return jnp.sum(jnp.where(square, jnp.broadcast_to(row, (INST, INST)), 0.0), axis=1, keepdims=True)

    def spread(column):
        return jnp.broadcast_to(column, (INST, LANES))

    def wait_all(copies):
        for c in copies:
            c.wait()

    def team_rows(which):
        return [
            remote(rows_t.at[which, yc], rows_t.at[which, yc], t_ss.at[which, k - 1], t_rs.at[which, k - 1], team_peer(k))
            for k in team_order
        ]

    def sum_team(which):
        total = rows_t[which, 0]
        for i in range(1, TEAM):
            total = total + rows_t[which, i]
        return total

    def far_row(which):
        return remote(rows_p.at[which], rows_pr.at[which], p_ss.at[which], p_rs.at[which], far_peer)

    def product(k):
        j = flip(x, k)
        out = jnp.dot(dbf_ref[...], m_ref[:, at(j, WIDE)], preferred_element_type=F32)
        if k:
            s1x[k - 1] = out[:HALF].astype(BF16)
        else:
            own0_ref[...] = out[:HALF]
        own1_ref[j] = out[HALF:]
        for q in near_last:
            s1z[q - 1, j] = own1_ref[j, :, at(flip(zl, q), CHUNK)].astype(BF16)

    def send_product(k):
        j = flip(x, k)
        sent_x = None
        if k:
            sent_x = remote(s1x.at[k - 1], r1x.at[k - 1], a_ss.at[0, k - 1], a_rs.at[0, k - 1], x_peer(k))
        sent_z = [
            remote(s1z.at[q - 1, j], r1z.at[q - 1, j], s_ss.at[q - 1, k], s_rs.at[q - 1, k], z_peer(q)) for q in near_last
        ]
        return sent_x, sent_z

    def scatter_dual():
        sends = {}
        for k in order:
            product(k)
            sends[k] = send_product(k)
        return sends

    def second_dual(sends):
        later = []

        def finish_z(k):
            j = flip(x, k)
            wait_all(sends[k][1])
            total = own1_ref[j, :, at(zl, CHUNK)]
            for q in range(3):
                total = total + r1z[q, j].astype(F32)
            if k:
                s2x[k - 1] = total.astype(BF16)
                later.append(remote(s2x.at[k - 1], r2x.at[k - 1], a_ss.at[3, k - 1], a_rs.at[3, k - 1], x_peer(k)))
            else:
                t1_ref[...] = total

        finish_z(2)
        finish_z(1)
        for k in (1, 2, 3):
            sends[k][0].wait()
        t0_ref[...] = own0_ref[...] + r1x[0].astype(F32) + r1x[1].astype(F32) + r1x[2].astype(F32)
        for k in near_last:
            s2z[k - 1] = t0_ref[:, at(flip(zl, k), CHUNK)].astype(BF16)
            later.append(remote(s2z.at[k - 1], r2z.at[k - 1], a_ss.at[2, k - 1], a_rs.at[2, k - 1], z_peer(k)))
        finish_z(3)
        finish_z(0)
        return later

    def gather_dual(later, process, aside=None):
        wait_all(later)
        upper = t0_ref[:, at(zl, CHUNK)] + r2z[0].astype(F32) + r2z[1].astype(F32) + r2z[2].astype(F32)
        lower = t1_ref[...] + r2x[0].astype(F32) + r2x[1].astype(F32) + r2x[2].astype(F32)
        gather[x, zl, :HALF] = upper.astype(BF16)
        gather[x, zl, HALF:] = lower.astype(BF16)
        mine = gather.at[x, zl]
        z_own = {}
        x_own = {}
        for k in near_last:
            z_own[k] = remote(mine, mine, a_ss.at[4, k - 1], a_rs.at[4, k - 1], z_peer(k))
            x_own[k] = remote(mine, mine, a_ss.at[5, k - 1], a_rs.at[5, k - 1], x_peer(k))
        process(x, zl)
        from_x = {}
        from_z = {}
        for k in (1, 3, 2):
            z_own[k].wait()
            part = gather.at[x, flip(zl, k), pl.ds(0, HALF)]
            for q in near_last:
                from_x[q, k] = remote(part, part, f_ss.at[0, k - 1, q - 1], f_rs.at[0, k - 1, q - 1], x_peer(q))
            x_own[k].wait()
            part = gather.at[flip(x, k), zl, pl.ds(HALF, HALF)]
            for q in near_last:
                from_z[k, q] = remote(part, part, f_ss.at[1, k - 1, q - 1], f_rs.at[1, k - 1, q - 1], z_peer(q))
            if k != 2:
                process(x, flip(zl, k))
                process(flip(x, k), zl)
        process(x, flip(zl, 2))
        process(flip(x, 2), zl)
        if aside is not None:
            aside()
        for qx, qz in ((1, 1), (3, 1), (1, 3), (3, 3), (2, 1), (1, 2), (2, 3), (3, 2), (2, 2)):
            from_x[qx, qz].wait()
            from_z[qx, qz].wait()
            process(flip(x, qx), flip(zl, qz))

    def halves(body):
        def process(gx, gz):
            for part in range(CHUNK // LANES):
                cols = at((gx * SIDE + gz) * (CHUNK // LANES) + part, LANES)
                image = gather[gx, gz, :, part * LANES : (part + 1) * LANES].astype(F32)
                body(image, cols)

        return process

    def with_product(body, rows, uses):
        done = halves(body)
        started = []

        def process(gx, gz):
            done(gx, gz)
            cols = at(gx * SIDE + gz, CHUNK)
            out = lax.dot_general(
                e_ref[rows, cols], m_ref[:, cols], (((1,), (1,)), ((), ())), preferred_element_type=F32
            )
            for n, u in enumerate(uses):
                for i in range(TEAM):
                    part = out[n * INST : (n + 1) * INST, i * PIECE : (i + 1) * PIECE]
                    if started:
                        z_ref[u, i] += part
                    else:
                        z_ref[u, i] = part
            started.append(True)

        return process

    def scatter_primal(u):
        sends = []
        for k in team_order:
            sb[u, k - 1] = z_ref[u, flip(yc, k)].astype(BF16)
            sends.append(remote(sb.at[u, k - 1], rb.at[u, k - 1], b_ss.at[u, k - 1], b_rs.at[u, k - 1], team_peer(k)))
        return sends

    def far_primal(u, sends):
        wait_all(sends)
        total = z_ref[u, yc]
        for k in range(1, TEAM):
            total = total + rb[u, k - 1].astype(F32)
        zs[u] = total.astype(BF16)
        return remote(zs.at[u], zr.at[u], z_ss.at[u], z_rs.at[u], far_peer)

    def done_primal(u, copy):
        copy.wait()
        return zs[u].astype(F32) + zr[u].astype(F32)

    def gather_primal(v):
        return [
            remote(gb.at[v, yc], gb.at[v, yc], g_ss.at[v, k - 1], g_rs.at[v, k - 1], team_peer(k)) for k in team_order
        ]

    def fill_dual(v):
        for i in range(TEAM):
            dbf_ref[:, i * PIECE : (i + 1) * PIECE] = gb[v, i]

    own_cols = at(yc, PIECE)

    load_d0.wait()
    dbf_ref[...] = d0_ref[...].astype(BF16)
    load_cp.wait()
    sum_ref[...] = jnp.zeros_like(sum_ref)

    def square_step(i, _):
        c = cp_ref[:, at(i, LANES)].astype(F32)
        sum_ref[...] += c * c
        return 0

    lax.fori_loop(0, COLS // LANES, square_step, 0, unroll=4)
    rows_t[0, yc] = to_row(jnp.sum(sum_ref[...], axis=1, keepdims=True))
    for position, k in enumerate(order):
        m_loads[position].wait()
        product(k)
    pl.semaphore_wait(barrier, 14)
    sends = {k: send_product(k) for k in order}
    norm_copies = team_rows(0)

    wait_all(small_loads)
    load_ct.wait()
    code = code_ref[...]
    half_code = code // 2
    low_ref[...] = -0.25 - 0.75 * (code - 2 * half_code).astype(F32)
    high_ref[...] = 0.25 + 0.75 * half_code.astype(F32)
    theta_ref[...] = spread(ratio(2))
    wait_all(norm_copies)
    rows_p[0] = sum_team(0)
    norm_far = far_row(0)
    later = second_dual(sends)
    norm_far.wait()
    norm_sum = to_column(rows_p[0] + rows_pr[0])
    scale = jnp.sqrt(norm_sum / VARS + EPS)
    tau_ref[...] = spread(ratio(0) / scale)
    sigma_ref[...] = spread(ratio(1) * scale)
    scale2_ref[...] = spread(VARS * scale * scale)

    def first_step(image, cols):
        reduced = cp_ref[:, cols].astype(F32) - image
        shifted = 0.0 - tau_ref[...] * reduced
        projected = jnp.minimum(jnp.maximum(shifted, low_ref[:, cols]), high_ref[:, cols])
        red0_ref[:, cols] = reduced
        sh0_ref[:, cols] = shifted
        e_ref[:INST, cols] = (projected + theta_ref[...] * projected).astype(BF16)

    gather_dual(later, with_product(first_step, slice(0, INST), (0,)))

    sends = scatter_primal(0)

    def slope_of(shifted, cols):
        return jax.nn.sigmoid(SHARP * (shifted - low_ref[:, cols])) * jax.nn.sigmoid(
            SHARP * (high_ref[:, cols] - shifted)
        )

    def slope_step(i, _):
        cols = at(i, LANES)
        slope = slope_of(sh0_ref[:, cols], cols)
        slope0_ref[:, cols] = slope
        e_ref[INST:, cols] = (slope * red0_ref[:, cols]).astype(BF16)
        return 0

    lax.fori_loop(0, COLS // LANES, slope_step, 0, unroll=2)
    far = far_primal(0, sends)
    for i in range(SIDE):
        out = lax.dot_general(
            e_ref[INST:, :], m_ref[i * 2 * PIECE : (i + 1) * 2 * PIECE, :], (((1,), (1,)), ((), ())),
            preferred_element_type=F32,
        )
        z_ref[1, 2 * i] = out[:, :PIECE]
        z_ref[1, 2 * i + 1] = out[:, PIECE:]
    image = done_primal(0, far)
    residue0 = right_ref[:, own_cols] - image
    dual1 = d0_ref[:, own_cols] + sigma_ref[...] * residue0
    gb[0, yc] = dual1.astype(BF16)
    gathers = gather_primal(0)
    weigh_sends = scatter_primal(1)
    dual1_ref[...] = dual1
    weigh_ref[...] = sigma_ref[...] * residue0
    wait_all(gathers)
    fill_dual(0)

    sends = scatter_dual()
    weigh_far = far_primal(1, weigh_sends)
    later = second_dual(sends)
    wimg_ref[...] = tau_ref[...] * (1.0 + theta_ref[...]) * sigma_ref[...] * done_primal(1, weigh_far)
    sum_ref[...] = jnp.zeros_like(sum_ref)

    def second_step(image, cols):
        low, high = low_ref[:, cols], high_ref[:, cols]
        reduced = cp_ref[:, cols].astype(F32) - image
        before = jnp.minimum(jnp.maximum(sh0_ref[:, cols], low), high)
        shifted = before - tau_ref[...] * reduced
        projected = jnp.minimum(jnp.maximum(shifted, low), high)
        primal_ref[:, cols] = projected
        e_ref[INST:, cols] = (projected + theta_ref[...] * (projected - before)).astype(BF16)
        slope_adj = slope_of(shifted, cols) * ct_ref[:, cols].astype(F32)
        sa1_ref[:, cols] = slope_adj
        e_ref[:INST, cols] = (tau_ref[...] * slope_adj).astype(BF16)
        sum_ref[...] += slope_adj * reduced + slope_adj * (slope0_ref[:, cols] * red0_ref[:, cols])

    gather_dual(later, with_product(second_step, slice(0, 2 * INST), (2, 3)))

    primal_copy = pltpu.make_async_copy(primal_ref, primal_out, out_sem.at[0])

    sends = scatter_primal(2)
    rows_t[1, yc] = to_row(tau_ref[:, 0:1] * jnp.sum(sum_ref[...], axis=1, keepdims=True))
    factor_copies = team_rows(1)
    primal_copy.start()
    far = far_primal(2, sends)
    end_sends = scatter_primal(3)
    wait_all(factor_copies)
    rows_p[1] = sum_team(1)
    factor_far = far_row(1)
    adjoint = done_primal(2, far)
    rounded = adjoint.astype(BF16)
    gb[1, yc] = rounded
    gathers = gather_primal(1)
    weighed = adjoint * weigh_ref[...] - rounded.astype(F32) * wimg_ref[...]
    rows_t[2, yc] = to_row(jnp.sum(weighed, axis=1, keepdims=True))
    factor_copies = team_rows(2)
    wait_all(gathers)
    fill_dual(1)

    sends = scatter_dual()
    end_far = far_primal(3, end_sends)
    wait_all(factor_copies)
    rowx[x] = sum_team(2)
    x_rows = [remote(rowx.at[x], rowx.at[x], rx_ss.at[k - 1], rx_rs.at[k - 1], x_peer(k)) for k in (1, 2, 3)]
    later = second_dual(sends)
    wait_all(x_rows)
    rowz[zl] = rowx[0] + rowx[1] + rowx[2] + rowx[3]
    z_rows = [remote(rowz.at[zl], rowz.at[zl], rz_ss.at[k - 1], rz_rs.at[k - 1], z_peer(k)) for k in (1, 2, 3)]
    factor_far.wait()
    residue1 = right_ref[:, own_cols] - done_primal(3, end_far)
    gd[yc] = dual1_ref[...] + sigma_ref[...] * residue1
    dual_gathers = [
        remote(gd.at[yc], gd.at[yc], gd_ss.at[k - 1], gd_rs.at[k - 1], team_peer(k)) for k in team_order
    ]
    wait_all(z_rows)
    factors = to_column(rows_p[1] + rows_pr[1] + (rowz[0] + rowz[1] + rowz[2] + rowz[3]))
    sum_ref[...] = spread(factors) / scale2_ref[...]

    def last_step(image, cols):
        slope_adj = sa1_ref[:, cols]
        ahead = slope_adj - (1.0 + theta_ref[...]) * (sigma_ref[...] * image)
        gradient = tau_ref[...] * (slope_adj + slope0_ref[:, cols] * ahead)
        grad_ref[:, cols] = cp_ref[:, cols].astype(F32) * sum_ref[...] - gradient

    grad_process = halves(last_step)
    out_copies = []

    def process(gx, gz):
        grad_process(gx, gz)
        cols = at(gx * SIDE + gz, CHUNK)
        copy = pltpu.make_async_copy(grad_ref.at[:, cols], grad_out.at[:, cols], out_sem.at[2 + len(out_copies)])
        copy.start()
        out_copies.append(copy)

    dual_copy = pltpu.make_async_copy(dual_ref, dual_out, out_sem.at[1])

    def dual_end():
        wait_all(dual_gathers)
        for i in range(TEAM):
            dual_ref[:, i * PIECE : (i + 1) * PIECE] = gd[i]
        dual_copy.start()

    gather_dual(later, process, dual_end)
    primal_copy.wait()
    dual_copy.wait()
    wait_all(out_copies)


def keep(a, b, c, out_a, out_b, out_c, sem):
    copies = [pltpu.make_async_copy(b, out_b, sem.at[8])]
    for n in range(4):
        rows = pl.ds(n * 16, 16)
        copies.append(pltpu.make_async_copy(a.at[rows], out_a.at[rows], sem.at[n]))
        copies.append(pltpu.make_async_copy(c.at[rows], out_c.at[rows], sem.at[4 + n]))
    for copy in copies:
        copy.start()
    for copy in copies:
        copy.wait()


def local(matrix, cost_pred, cost_true, dual_start, right_side, bound_code, step_numer, step_denom):
    dma = pltpu.SemaphoreType.DMA
    v = pltpu.VMEM
    anywhere = pl.BlockSpec(memory_space=pl.ANY)
    uses, rows = 4, 3
    scratch = [
        v((INST, COLS), F32), v((INST, ROWS), F32), v((INST, COLS), F32), dma((2 + SIDE * SIDE,)),
        v((ROWS, COLS), BF16), dma((SIDE,)), v((INST, COLS), BF16), v((INST, COLS), BF16), v((INST, ROWS), F32),
        v((1, ROWS), F32), v((1, COLS), jnp.int32), v((3, INST), jnp.int32), v((3, INST), jnp.int32), dma((7,)),
        v((INST, LANES), F32), v((INST, LANES), F32), v((INST, LANES), F32), v((INST, LANES), F32),
        v((1, COLS), F32), v((1, COLS), F32), v((INST, LANES), F32),
        v((INST, ROWS), BF16), v((HALF, WIDE), F32), v((SIDE, HALF, WIDE), F32), v((HALF, WIDE), F32),
        v((HALF, CHUNK), F32), v((INST, COLS), F32), v((INST, COLS), F32), v((INST, COLS), F32),
        v((INST, COLS), F32), v((2 * INST, COLS), BF16), v((uses, TEAM, INST, PIECE), F32),
        v((3, HALF, WIDE), BF16), v((3, SIDE, HALF, CHUNK), BF16), v((3, HALF, WIDE), BF16), v((3, SIDE, HALF, CHUNK), BF16),
        v((3, HALF, CHUNK), BF16), v((3, HALF, CHUNK), BF16), v((3, HALF, CHUNK), BF16), v((3, HALF, CHUNK), BF16),
        v((SIDE, SIDE, INST, CHUNK), BF16),
        dma((6, 3)), dma((6, 3)), dma((3, SIDE)), dma((3, SIDE)), dma((2, 3, 3)), dma((2, 3, 3)),
        v((uses, TEAM - 1, INST, PIECE), BF16), v((uses, TEAM - 1, INST, PIECE), BF16),
        v((uses, INST, PIECE), BF16), v((uses, INST, PIECE), BF16),
        v((2, TEAM, INST, PIECE), BF16), v((TEAM, INST, PIECE), F32),
        dma((uses, TEAM - 1)), dma((uses, TEAM - 1)), dma((uses,)), dma((uses,)),
        dma((2, TEAM - 1)), dma((2, TEAM - 1)), dma((TEAM - 1,)), dma((TEAM - 1,)),
        v((rows, TEAM, 8, LANES), F32), v((2, 8, LANES), F32), v((2, 8, LANES), F32), v((SIDE, 8, LANES), F32),
        v((SIDE, 8, LANES), F32),
        dma((rows, TEAM - 1)), dma((rows, TEAM - 1)), dma((2,)), dma((2,)), dma((3,)), dma((3,)), dma((3,)), dma((3,)),
        v((INST, PIECE), F32), v((INST, PIECE), F32), v((INST, PIECE), F32),
    ]
    outs = (
        jax.ShapeDtypeStruct((INST, COLS), F32),
        jax.ShapeDtypeStruct((INST, ROWS), F32),
        jax.ShapeDtypeStruct((INST, COLS), F32),
    )
    results = pl.pallas_call(
        kernel,
        out_shape=outs,
        in_specs=[anywhere] * 8,
        out_specs=(anywhere,) * 3,
        scratch_shapes=scratch,
        compiler_params=pltpu.CompilerParams(
            collective_id=0, has_side_effects=True, vmem_limit_bytes=63 * 2**20
        ),
    )(
        matrix,
        cost_pred,
        cost_true,
        dual_start,
        right_side.reshape(1, ROWS),
        bound_code.reshape(1, COLS),
        step_numer.T,
        step_denom.T,
    )
    return pl.pallas_call(
        keep,
        out_shape=outs,
        in_specs=[anywhere] * 3,
        out_specs=(anywhere,) * 3,
        scratch_shapes=[dma((9,))],
        compiler_params=pltpu.CompilerParams(vmem_limit_bytes=63 * 2**20),
    )(*results)


def solution(mesh):
    placed = (
        P("rows", "cols"),
        P(None, "cols"),
        P(None, "cols"),
        P(None, "rows"),
        P("rows"),
        P("cols"),
        P(),
        P(),
    )
    return jax.shard_map(
        local,
        mesh=mesh,
        in_specs=placed,
        out_specs=(P(None, "cols"), P(None, "rows"), P(None, "cols")),
        check_vma=False,
    )
```

```python
import jax
import jax.numpy as jnp
from jax import lax
from jax.experimental import pallas as pl
from jax.experimental.pallas import tpu as pltpu
from jax.sharding import PartitionSpec as P

VARS = 65536
MESH = pl.DeviceIdType.MESH
F32 = jnp.float32
BF16 = jnp.bfloat16
SHARP = 16.0
EPS = 1e-06

INST = 64
CUT = 80
ROWS = 1024
COLS = 4096
SIDE = 4
WIDE = COLS // SIDE
CHUNK = WIDE // SIDE
TEAM = 8
PIECE = ROWS // TEAM
LANES = 128
STACK = INST * CHUNK // LANES
REST = STACK - CUT


def kernel(
    m_hbm, cp_hbm, ct_hbm, d0_hbm, right_hbm, code_hbm, numer_hbm, denom_hbm,
    primal_out, dual_out, grad_out,
    primal_ref, dual_ref, grad_ref, out_sem, m_ref, m_sem, cp_ref, ct_ref, d0_ref, right_ref, code_ref, numer_ref, denom_ref, in_sem,
    tau_ref, sigma_ref, theta_ref, scale2_ref, low_ref, high_ref, sum_ref,
    dbf_ref, own_ref, t0_ref, t1_ref, red0_ref, sh0_ref, slope0_ref, sa1_ref, e_ref, z_ref,
    s1x, s1z, r1x, r1z, s2z, s2x, r2z, r2x, gather,
    a_ss, a_rs, s_ss, s_rs, f_ss, f_rs,
    sb, rb, zs, zr, gb, gd,
    b_ss, b_rs, z_ss, z_rs, g_ss, g_rs, gd_ss, gd_rs,
    rows_t, rows_p, rows_pr, rowx, rowz,
    t_ss, t_rs, p_ss, p_rs, rx_ss, rx_rs, rz_ss, rz_rs,
    dual1_ref, weigh_ref, wimg_ref,
):
    rr = lax.axis_index("rows")
    cc = lax.axis_index("cols")
    x, zl = rr // SIDE, lax.rem(rr, SIDE)
    zh, yc = cc // TEAM, lax.rem(cc, TEAM)
    y = yc // 2

    def flip(value, k):
        if k == 0:
            return value
        total = value
        for bit in (1, 2, 4):
            if k & bit:
                total = total + bit - 2 * bit * lax.rem(value // bit, 2)
        return total

    def x_peer(k):
        return (flip(x, k) * SIDE + zl, cc)

    def z_peer(k):
        return (x * SIDE + flip(zl, k), cc)

    def team_peer(k):
        return (rr, zh * TEAM + flip(yc, k))

    far_peer = (rr, (1 - zh) * TEAM + yc)

    def remote(src, dst, send, recv, peer):
        copy = pltpu.make_async_remote_copy(
            src_ref=src, dst_ref=dst, send_sem=send, recv_sem=recv, device_id=peer, device_id_type=MESH
        )
        copy.start()
        return copy

    def at(value, size):
        return pl.ds(pl.multiple_of(value * size, size), size)

    order = (2, 1, 3, 0)
    near_last = (2, 3, 1)
    team_order = (4, 5, 6, 7, 2, 3, 1)

    def load(n, src, dst):
        copy = pltpu.make_async_copy(src, dst, in_sem.at[n])
        copy.start()
        return copy

    load_d0 = load(0, d0_hbm, d0_ref)
    load_cp = load(1, cp_hbm, cp_ref)
    m_loads = []
    for k in order:
        cols = at(flip(x, k), WIDE)
        copy = pltpu.make_async_copy(m_hbm.at[:, cols], m_ref.at[:, cols], m_sem.at[k])
        copy.start()
        m_loads.append(copy)
    small_loads = [
        load(2, right_hbm, right_ref), load(3, code_hbm, code_ref),
        load(4, numer_hbm, numer_ref), load(5, denom_hbm, denom_ref),
    ]
    load_ct = load(6, ct_hbm, ct_ref)

    barrier = pltpu.get_barrier_semaphore()
    for k in (1, 2, 3):
        pl.semaphore_signal(barrier, inc=1, device_id=x_peer(k), device_id_type=MESH)
        pl.semaphore_signal(barrier, inc=1, device_id=z_peer(k), device_id_type=MESH)
    for k in range(1, TEAM):
        pl.semaphore_signal(barrier, inc=1, device_id=team_peer(k), device_id_type=MESH)
    pl.semaphore_signal(barrier, inc=1, device_id=far_peer, device_id_type=MESH)

    lane = lax.broadcasted_iota(jnp.int32, (INST, LANES), 1)
    diagonal = lane == lax.broadcasted_iota(jnp.int32, (INST, LANES), 0)

    def to_row(column):
        spread = jnp.where(diagonal, jnp.broadcast_to(column, (INST, LANES)), 0.0)
        return jnp.broadcast_to(jnp.sum(spread, axis=0, keepdims=True), (8, LANES))

    def to_column(row):
        spread = jnp.where(diagonal, jnp.broadcast_to(row[0:1, :], (INST, LANES)), 0.0)
        return jnp.sum(spread, axis=1, keepdims=True)

    square = lax.broadcasted_iota(jnp.int32, (INST, INST), 1) == lax.broadcasted_iota(jnp.int32, (INST, INST), 0)

    def ratio(n):
        row = numer_ref[n : n + 1, :].astype(F32) / denom_ref[n : n + 1, :].astype(F32)
        return jnp.sum(jnp.where(square, jnp.broadcast_to(row, (INST, INST)), 0.0), axis=1, keepdims=True)

    def spread(column):
        return jnp.broadcast_to(column, (INST, LANES))

    def wait_all(copies):
        for c in copies:
            c.wait()

    def team_rows(which):
        return [
            remote(rows_t.at[which, yc], rows_t.at[which, yc], t_ss.at[which, k - 1], t_rs.at[which, k - 1], team_peer(k))
            for k in team_order
        ]

    def sum_team(which):
        total = rows_t[which, 0]
        for i in range(1, TEAM):
            total = total + rows_t[which, i]
        return total

    def far_row(which):
        return remote(rows_p.at[which], rows_pr.at[which], p_ss.at[which], p_rs.at[which], far_peer)

    def product(k):
        j = flip(x, k)
        out = jnp.dot(dbf_ref[...], m_ref[:, at(j, WIDE)], preferred_element_type=F32)
        for gz in range(SIDE):
            for part in range(CHUNK // LANES):
                start = gz * CHUNK + part * LANES
                own_ref[j, gz, part * INST : (part + 1) * INST] = out[:, start : start + LANES]
        if k:
            s1x[k - 1] = own_ref[j, :, :CUT].astype(BF16)
        for q in near_last:
            s1z[q - 1, j] = own_ref[j, flip(zl, q), CUT:].astype(BF16)

    def send_product(k):
        j = flip(x, k)
        sent_x = None
        if k:
            sent_x = remote(s1x.at[k - 1], r1x.at[k - 1], a_ss.at[0, k - 1], a_rs.at[0, k - 1], x_peer(k))
        sent_z = [
            remote(s1z.at[q - 1, j], r1z.at[q - 1, j], s_ss.at[q - 1, k], s_rs.at[q - 1, k], z_peer(q)) for q in near_last
        ]
        return sent_x, sent_z

    def scatter_dual():
        sends = {}
        for k in order:
            product(k)
            sends[k] = send_product(k)
        return sends

    def second_dual(sends):
        later = []

        def finish_z(k):
            j = flip(x, k)
            wait_all(sends[k][1])
            total = own_ref[j, zl, CUT:]
            for q in range(3):
                total = total + r1z[q, j].astype(F32)
            if k:
                s2x[k - 1] = total.astype(BF16)
                later.append(remote(s2x.at[k - 1], r2x.at[k - 1], a_ss.at[3, k - 1], a_rs.at[3, k - 1], x_peer(k)))
            else:
                t1_ref[...] = total

        finish_z(2)
        finish_z(1)
        for k in (1, 2, 3):
            sends[k][0].wait()
        t0_ref[...] = own_ref[x, :, :CUT] + r1x[0].astype(F32) + r1x[1].astype(F32) + r1x[2].astype(F32)
        for k in near_last:
            s2z[k - 1] = t0_ref[flip(zl, k)].astype(BF16)
            later.append(remote(s2z.at[k - 1], r2z.at[k - 1], a_ss.at[2, k - 1], a_rs.at[2, k - 1], z_peer(k)))
        finish_z(3)
        finish_z(0)
        return later

    def gather_dual(later, process, aside=None):
        wait_all(later)
        upper = t0_ref[zl] + r2z[0].astype(F32) + r2z[1].astype(F32) + r2z[2].astype(F32)
        lower = t1_ref[...] + r2x[0].astype(F32) + r2x[1].astype(F32) + r2x[2].astype(F32)
        gather[x, zl, :CUT] = upper.astype(BF16)
        gather[x, zl, CUT:] = lower.astype(BF16)
        above = pl.ds(0, CUT)
        below = pl.ds(CUT, REST)
        mine_above = gather.at[x, zl, above]
        mine_below = gather.at[x, zl, below]
        z_own = {}
        x_own = {}
        z_more = {}
        x_more = {}
        for k in near_last:
            z_own[k] = remote(mine_above, mine_above, a_ss.at[4, k - 1], a_rs.at[4, k - 1], z_peer(k))
            x_own[k] = remote(mine_below, mine_below, a_ss.at[5, k - 1], a_rs.at[5, k - 1], x_peer(k))
        for k in near_last:
            z_more[k] = remote(mine_below, mine_below, a_ss.at[6, k - 1], a_rs.at[6, k - 1], z_peer(k))
            x_more[k] = remote(mine_above, mine_above, a_ss.at[7, k - 1], a_rs.at[7, k - 1], x_peer(k))
        process(x, zl)
        from_x = {}
        from_z = {}
        for k in (1, 3, 2):
            x_own[k].wait()
            part = gather.at[flip(x, k), zl, below]
            for q in near_last:
                from_z[k, q] = remote(part, part, f_ss.at[1, k - 1, q - 1], f_rs.at[1, k - 1, q - 1], z_peer(q))
            z_own[k].wait()
            part = gather.at[x, flip(zl, k), above]
            for q in near_last:
                from_x[q, k] = remote(part, part, f_ss.at[0, k - 1, q - 1], f_rs.at[0, k - 1, q - 1], x_peer(q))
        for k in (1, 3, 2):
            z_more[k].wait()
            process(x, flip(zl, k))
            x_more[k].wait()
            process(flip(x, k), zl)
        if aside is not None:
            aside()
        for qx, qz in ((1, 1), (3, 1), (1, 3), (3, 3), (2, 1), (1, 2), (2, 3), (3, 2), (2, 2)):
            from_x[qx, qz].wait()
            from_z[qx, qz].wait()
            process(flip(x, qx), flip(zl, qz))

    def halves(body):
        def process(gx, gz):
            for part in range(CHUNK // LANES):
                cols = at((gx * SIDE + gz) * (CHUNK // LANES) + part, LANES)
                image = gather[gx, gz, part * INST : (part + 1) * INST].astype(F32)
                body(image, cols)

        return process

    def with_product(body, rows, uses):
        done = halves(body)
        started = []

        def process(gx, gz):
            done(gx, gz)
            cols = at(gx * SIDE + gz, CHUNK)
            out = lax.dot_general(
                e_ref[rows, cols], m_ref[:, cols], (((1,), (1,)), ((), ())), preferred_element_type=F32
            )
            for n, u in enumerate(uses):
                for i in range(TEAM):
                    part = out[n * INST : (n + 1) * INST, i * PIECE : (i + 1) * PIECE]
                    if started:
                        z_ref[u, i] += part
                    else:
                        z_ref[u, i] = part
            started.append(True)

        return process

    def scatter_primal(u):
        sends = []
        for k in team_order:
            sb[u, k - 1] = z_ref[u, flip(yc, k)].astype(BF16)
            sends.append(remote(sb.at[u, k - 1], rb.at[u, k - 1], b_ss.at[u, k - 1], b_rs.at[u, k - 1], team_peer(k)))
        return sends

    def far_primal(u, sends):
        wait_all(sends)
        total = z_ref[u, yc]
        for k in range(1, TEAM):
            total = total + rb[u, k - 1].astype(F32)
        zs[u] = total.astype(BF16)
        return remote(zs.at[u], zr.at[u], z_ss.at[u], z_rs.at[u], far_peer)

    def done_primal(u, copy):
        copy.wait()
        return zs[u].astype(F32) + zr[u].astype(F32)

    def gather_primal(v):
        return [
            remote(gb.at[v, yc], gb.at[v, yc], g_ss.at[v, k - 1], g_rs.at[v, k - 1], team_peer(k)) for k in team_order
        ]

    def fill_dual(v):
        for i in range(TEAM):
            dbf_ref[:, i * PIECE : (i + 1) * PIECE] = gb[v, i]

    own_cols = at(yc, PIECE)

    load_d0.wait()
    dbf_ref[...] = d0_ref[...].astype(BF16)
    load_cp.wait()
    sum_ref[...] = jnp.zeros_like(sum_ref)

    def square_step(i, _):
        c = cp_ref[:, at(i, LANES)].astype(F32)
        sum_ref[...] += c * c
        return 0

    lax.fori_loop(0, COLS // LANES, square_step, 0, unroll=4)
    rows_t[0, yc] = to_row(jnp.sum(sum_ref[...], axis=1, keepdims=True))
    for position, k in enumerate(order):
        m_loads[position].wait()
        product(k)
    pl.semaphore_wait(barrier, 14)
    sends = {k: send_product(k) for k in order}
    norm_copies = team_rows(0)

    wait_all(small_loads)
    load_ct.wait()
    code = code_ref[...]
    half_code = code // 2
    low_ref[...] = -0.25 - 0.75 * (code - 2 * half_code).astype(F32)
    high_ref[...] = 0.25 + 0.75 * half_code.astype(F32)
    theta_ref[...] = spread(ratio(2))
    wait_all(norm_copies)
    rows_p[0] = sum_team(0)
    norm_far = far_row(0)
    later = second_dual(sends)
    norm_far.wait()
    norm_sum = to_column(rows_p[0] + rows_pr[0])
    scale = jnp.sqrt(norm_sum / VARS + EPS)
    tau_ref[...] = spread(ratio(0) / scale)
    sigma_ref[...] = spread(ratio(1) * scale)
    scale2_ref[...] = spread(VARS * scale * scale)

    def first_step(image, cols):
        reduced = cp_ref[:, cols].astype(F32) - image
        shifted = 0.0 - tau_ref[...] * reduced
        projected = jnp.minimum(jnp.maximum(shifted, low_ref[:, cols]), high_ref[:, cols])
        red0_ref[:, cols] = reduced
        sh0_ref[:, cols] = shifted
        e_ref[:INST, cols] = (projected + theta_ref[...] * projected).astype(BF16)

    gather_dual(later, with_product(first_step, slice(0, INST), (0,)))

    sends = scatter_primal(0)

    def slope_of(shifted, cols):
        return jax.nn.sigmoid(SHARP * (shifted - low_ref[:, cols])) * jax.nn.sigmoid(
            SHARP * (high_ref[:, cols] - shifted)
        )

    def slope_step(i, _):
        cols = at(i, LANES)
        slope = slope_of(sh0_ref[:, cols], cols)
        slope0_ref[:, cols] = slope
        e_ref[INST:, cols] = (slope * red0_ref[:, cols]).astype(BF16)
        return 0

    lax.fori_loop(0, COLS // LANES, slope_step, 0, unroll=2)
    far = far_primal(0, sends)
    for i in range(SIDE):
        out = lax.dot_general(
            e_ref[INST:, :], m_ref[i * 2 * PIECE : (i + 1) * 2 * PIECE, :], (((1,), (1,)), ((), ())),
            preferred_element_type=F32,
        )
        z_ref[1, 2 * i] = out[:, :PIECE]
        z_ref[1, 2 * i + 1] = out[:, PIECE:]
    weigh_sends = scatter_primal(1)
    image = done_primal(0, far)
    residue0 = right_ref[:, own_cols] - image
    dual1 = d0_ref[:, own_cols] + sigma_ref[...] * residue0
    gb[0, yc] = dual1.astype(BF16)
    gathers = gather_primal(0)
    dual1_ref[...] = dual1
    weigh_ref[...] = sigma_ref[...] * residue0
    wait_all(gathers)
    fill_dual(0)

    sends = scatter_dual()
    weigh_far = far_primal(1, weigh_sends)
    later = second_dual(sends)
    wimg_ref[...] = tau_ref[...] * (1.0 + theta_ref[...]) * sigma_ref[...] * done_primal(1, weigh_far)
    sum_ref[...] = jnp.zeros_like(sum_ref)

    def second_step(image, cols):
        low, high = low_ref[:, cols], high_ref[:, cols]
        reduced = cp_ref[:, cols].astype(F32) - image
        before = jnp.minimum(jnp.maximum(sh0_ref[:, cols], low), high)
        shifted = before - tau_ref[...] * reduced
        projected = jnp.minimum(jnp.maximum(shifted, low), high)
        primal_ref[:, cols] = projected
        e_ref[INST:, cols] = (projected + theta_ref[...] * (projected - before)).astype(BF16)
        slope_adj = slope_of(shifted, cols) * ct_ref[:, cols].astype(F32)
        sa1_ref[:, cols] = slope_adj
        e_ref[:INST, cols] = (tau_ref[...] * slope_adj).astype(BF16)
        sum_ref[...] += slope_adj * reduced + slope_adj * (slope0_ref[:, cols] * red0_ref[:, cols])

    gather_dual(later, with_product(second_step, slice(0, 2 * INST), (2, 3)))

    primal_copy = pltpu.make_async_copy(primal_ref, primal_out, out_sem.at[0])

    sends = scatter_primal(2)
    rows_t[1, yc] = to_row(tau_ref[:, 0:1] * jnp.sum(sum_ref[...], axis=1, keepdims=True))
    factor_copies = team_rows(1)
    primal_copy.start()
    far = far_primal(2, sends)
    end_sends = scatter_primal(3)
    wait_all(factor_copies)
    rows_p[1] = sum_team(1)
    factor_far = far_row(1)
    adjoint = done_primal(2, far)
    rounded = adjoint.astype(BF16)
    gb[1, yc] = rounded
    gathers = gather_primal(1)
    weighed = adjoint * weigh_ref[...] - rounded.astype(F32) * wimg_ref[...]
    rows_t[2, yc] = to_row(jnp.sum(weighed, axis=1, keepdims=True))
    factor_copies = team_rows(2)
    wait_all(gathers)
    fill_dual(1)

    sends = scatter_dual()
    end_far = far_primal(3, end_sends)
    wait_all(factor_copies)
    rowx[x] = sum_team(2)
    x_rows = [remote(rowx.at[x], rowx.at[x], rx_ss.at[k - 1], rx_rs.at[k - 1], x_peer(k)) for k in (1, 2, 3)]
    later = second_dual(sends)
    wait_all(x_rows)
    rowz[zl] = rowx[0] + rowx[1] + rowx[2] + rowx[3]
    z_rows = [remote(rowz.at[zl], rowz.at[zl], rz_ss.at[k - 1], rz_rs.at[k - 1], z_peer(k)) for k in (1, 2, 3)]
    factor_far.wait()
    residue1 = right_ref[:, own_cols] - done_primal(3, end_far)
    gd[yc] = dual1_ref[...] + sigma_ref[...] * residue1
    dual_gathers = [
        remote(gd.at[yc], gd.at[yc], gd_ss.at[k - 1], gd_rs.at[k - 1], team_peer(k)) for k in team_order
    ]
    wait_all(z_rows)
    factors = to_column(rows_p[1] + rows_pr[1] + (rowz[0] + rowz[1] + rowz[2] + rowz[3]))
    sum_ref[...] = spread(factors) / scale2_ref[...]

    def last_step(image, cols):
        slope_adj = sa1_ref[:, cols]
        ahead = slope_adj - (1.0 + theta_ref[...]) * (sigma_ref[...] * image)
        gradient = tau_ref[...] * (slope_adj + slope0_ref[:, cols] * ahead)
        grad_ref[:, cols] = cp_ref[:, cols].astype(F32) * sum_ref[...] - gradient

    grad_process = halves(last_step)
    out_copies = []

    def process(gx, gz):
        grad_process(gx, gz)
        cols = at(gx * SIDE + gz, CHUNK)
        copy = pltpu.make_async_copy(grad_ref.at[:, cols], grad_out.at[:, cols], out_sem.at[2 + len(out_copies)])
        copy.start()
        out_copies.append(copy)

    dual_copy = pltpu.make_async_copy(dual_ref, dual_out, out_sem.at[1])

    def dual_end():
        wait_all(dual_gathers)
        for i in range(TEAM):
            dual_ref[:, i * PIECE : (i + 1) * PIECE] = gd[i]
        dual_copy.start()

    gather_dual(later, process, dual_end)
    primal_copy.wait()
    dual_copy.wait()
    wait_all(out_copies)


def keep(a, b, c, out_a, out_b, out_c, hold_a, hold_b, hold_c, in_sem, out_sem):
    ways = [(b, hold_b, out_b)]
    for n in range(4):
        rows = pl.ds(n * 16, 16)
        ways.append((a.at[rows], hold_a.at[rows], out_a.at[rows]))
        ways.append((c.at[rows], hold_c.at[rows], out_c.at[rows]))
    loads = [pltpu.make_async_copy(src, hold, in_sem.at[n]) for n, (src, hold, _) in enumerate(ways)]
    stores = [pltpu.make_async_copy(hold, dst, out_sem.at[n]) for n, (_, hold, dst) in enumerate(ways)]
    for copy in loads:
        copy.start()
    for load, store in zip(loads, stores):
        load.wait()
        store.start()
    for copy in stores:
        copy.wait()


def local(matrix, cost_pred, cost_true, dual_start, right_side, bound_code, step_numer, step_denom):
    dma = pltpu.SemaphoreType.DMA
    v = pltpu.VMEM
    anywhere = pl.BlockSpec(memory_space=pl.ANY)
    uses, rows = 4, 3
    scratch = [
        v((INST, COLS), F32), v((INST, ROWS), F32), v((INST, COLS), F32), dma((2 + SIDE * SIDE,)),
        v((ROWS, COLS), BF16), dma((SIDE,)), v((INST, COLS), BF16), v((INST, COLS), BF16), v((INST, ROWS), F32),
        v((1, ROWS), F32), v((1, COLS), jnp.int32), v((3, INST), jnp.int32), v((3, INST), jnp.int32), dma((7,)),
        v((INST, LANES), F32), v((INST, LANES), F32), v((INST, LANES), F32), v((INST, LANES), F32),
        v((1, COLS), F32), v((1, COLS), F32), v((INST, LANES), F32),
        v((INST, ROWS), BF16), v((SIDE, SIDE, STACK, LANES), F32), v((SIDE, CUT, LANES), F32), v((REST, LANES), F32),
        v((INST, COLS), F32), v((INST, COLS), F32), v((INST, COLS), F32),
        v((INST, COLS), F32), v((2 * INST, COLS), BF16), v((uses, TEAM, INST, PIECE), F32),
        v((3, SIDE, CUT, LANES), BF16), v((3, SIDE, REST, LANES), BF16), v((3, SIDE, CUT, LANES), BF16),
        v((3, SIDE, REST, LANES), BF16), v((3, CUT, LANES), BF16), v((3, REST, LANES), BF16), v((3, CUT, LANES), BF16),
        v((3, REST, LANES), BF16), v((SIDE, SIDE, STACK, LANES), BF16),
        dma((8, 3)), dma((8, 3)), dma((3, SIDE)), dma((3, SIDE)), dma((2, 3, 3)), dma((2, 3, 3)),
        v((uses, TEAM - 1, INST, PIECE), BF16), v((uses, TEAM - 1, INST, PIECE), BF16),
        v((uses, INST, PIECE), BF16), v((uses, INST, PIECE), BF16),
        v((2, TEAM, INST, PIECE), BF16), v((TEAM, INST, PIECE), F32),
        dma((uses, TEAM - 1)), dma((uses, TEAM - 1)), dma((uses,)), dma((uses,)),
        dma((2, TEAM - 1)), dma((2, TEAM - 1)), dma((TEAM - 1,)), dma((TEAM - 1,)),
        v((rows, TEAM, 8, LANES), F32), v((2, 8, LANES), F32), v((2, 8, LANES), F32), v((SIDE, 8, LANES), F32),
        v((SIDE, 8, LANES), F32),
        dma((rows, TEAM - 1)), dma((rows, TEAM - 1)), dma((2,)), dma((2,)), dma((3,)), dma((3,)), dma((3,)), dma((3,)),
        v((INST, PIECE), F32), v((INST, PIECE), F32), v((INST, PIECE), F32),
    ]
    outs = (
        jax.ShapeDtypeStruct((INST, COLS), F32),
        jax.ShapeDtypeStruct((INST, ROWS), F32),
        jax.ShapeDtypeStruct((INST, COLS), F32),
    )
    results = pl.pallas_call(
        kernel,
        out_shape=outs,
        in_specs=[anywhere] * 8,
        out_specs=(anywhere,) * 3,
        scratch_shapes=scratch,
        compiler_params=pltpu.CompilerParams(
            collective_id=0, has_side_effects=True, vmem_limit_bytes=63 * 2**20
        ),
    )(
        matrix,
        cost_pred,
        cost_true,
        dual_start,
        right_side.reshape(1, ROWS),
        bound_code.reshape(1, COLS),
        step_numer.T,
        step_denom.T,
    )
    return pl.pallas_call(
        keep,
        out_shape=outs,
        in_specs=[anywhere] * 3,
        out_specs=(anywhere,) * 3,
        scratch_shapes=[v((INST, COLS), F32), v((INST, ROWS), F32), v((INST, COLS), F32), dma((9,)), dma((9,))],
        compiler_params=pltpu.CompilerParams(vmem_limit_bytes=63 * 2**20),
    )(*results)


def solution(mesh):
    placed = (
        P("rows", "cols"),
        P(None, "cols"),
        P(None, "cols"),
        P(None, "rows"),
        P("rows"),
        P("cols"),
        P(),
        P(),
    )
    return jax.shard_map(
        local,
        mesh=mesh,
        in_specs=placed,
        out_specs=(P(None, "cols"), P(None, "rows"), P(None, "cols")),
        check_vma=False,
    )
```

```python
import jax
import jax.numpy as jnp
from jax import lax
from jax.experimental import pallas as pl
from jax.experimental.pallas import tpu as pltpu
from jax.sharding import PartitionSpec as P

VARS = 65536
MESH = pl.DeviceIdType.MESH
F32 = jnp.float32
BF16 = jnp.bfloat16
SHARP = 16.0
EPS = 1e-06

INST = 64
CUT = 80
ROWS = 1024
COLS = 4096
SIDE = 4
WIDE = COLS // SIDE
CHUNK = WIDE // SIDE
TEAM = 8
PIECE = ROWS // TEAM
LANES = 128
CUT_OUT = 96
STACK = INST * CHUNK // LANES
REST = STACK - CUT


def kernel(
    m_hbm, cp_hbm, ct_hbm, d0_hbm, right_hbm, code_hbm, numer_hbm, denom_hbm,
    primal_out, dual_out, grad_out,
    primal_ref, dual_ref, grad_ref, out_sem, m_ref, m_sem, cp_ref, ct_ref, d0_ref, right_ref, code_ref, numer_ref, denom_ref, in_sem,
    tau_ref, sigma_ref, theta_ref, scale2_ref, low_ref, high_ref, sum_ref,
    dbf_ref, own_ref, t0_ref, t1_ref, red0_ref, sh0_ref, slope0_ref, sa1_ref, e_ref, z_ref,
    s1x, s1z, r1x, r1z, s2z, s2x, r2z, r2x, gather,
    a_ss, a_rs, s_ss, s_rs, f_ss, f_rs,
    sb, rb, zs, zr, gb, gd,
    b_ss, b_rs, z_ss, z_rs, g_ss, g_rs, gd_ss, gd_rs,
    rows_t, rows_p, rows_pr, rowx, rowz,
    t_ss, t_rs, p_ss, p_rs, rx_ss, rx_rs, rz_ss, rz_rs,
    dual1_ref, weigh_ref, wimg_ref, far_in,
):
    rr = lax.axis_index("rows")
    cc = lax.axis_index("cols")
    x, zl = rr // SIDE, lax.rem(rr, SIDE)
    zh, yc = cc // TEAM, lax.rem(cc, TEAM)
    y = yc // 2

    def flip(value, k):
        if k == 0:
            return value
        total = value
        for bit in (1, 2, 4):
            if k & bit:
                total = total + bit - 2 * bit * lax.rem(value // bit, 2)
        return total

    def x_peer(k):
        return (flip(x, k) * SIDE + zl, cc)

    def z_peer(k):
        return (x * SIDE + flip(zl, k), cc)

    def team_peer(k):
        return (rr, zh * TEAM + flip(yc, k))

    far_peer = (rr, (1 - zh) * TEAM + yc)

    def remote(src, dst, send, recv, peer):
        copy = pltpu.make_async_remote_copy(
            src_ref=src, dst_ref=dst, send_sem=send, recv_sem=recv, device_id=peer, device_id_type=MESH
        )
        copy.start()
        return copy

    def at(value, size):
        return pl.ds(pl.multiple_of(value * size, size), size)

    order = (2, 1, 3, 0)
    near_last = (2, 3, 1)
    far_pieces = ((1, 1), (3, 1), (1, 3), (3, 3), (2, 1), (1, 2), (2, 3), (3, 2), (2, 2))
    team_order = (4, 5, 6, 7, 2, 3, 1)

    def load(n, src, dst):
        copy = pltpu.make_async_copy(src, dst, in_sem.at[n])
        copy.start()
        return copy

    load_d0 = load(0, d0_hbm, d0_ref)
    load_cp = load(1, cp_hbm, cp_ref)
    m_loads = []
    for k in order:
        cols = at(flip(x, k), WIDE)
        copy = pltpu.make_async_copy(m_hbm.at[:, cols], m_ref.at[:, cols], m_sem.at[k])
        copy.start()
        m_loads.append(copy)
    small_loads = [
        load(2, right_hbm, right_ref), load(3, code_hbm, code_ref),
        load(4, numer_hbm, numer_ref), load(5, denom_hbm, denom_ref),
    ]
    load_ct = load(6, ct_hbm, ct_ref)

    barrier = pltpu.get_barrier_semaphore()
    for k in (1, 2, 3):
        pl.semaphore_signal(barrier, inc=1, device_id=x_peer(k), device_id_type=MESH)
        pl.semaphore_signal(barrier, inc=1, device_id=z_peer(k), device_id_type=MESH)
    for k in range(1, TEAM):
        pl.semaphore_signal(barrier, inc=1, device_id=team_peer(k), device_id_type=MESH)

    border = 1 - lax.rem((zl + 1) // 2, 2)
    across = (x * SIDE + (SIDE - 1 - zl), (1 - zh) * TEAM + yc)

    @pl.when(border == 1)
    def _():
        pl.semaphore_signal(barrier, inc=1, device_id=across, device_id_type=MESH)


    lane = lax.broadcasted_iota(jnp.int32, (INST, LANES), 1)
    diagonal = lane == lax.broadcasted_iota(jnp.int32, (INST, LANES), 0)

    def to_row(column):
        spread = jnp.where(diagonal, jnp.broadcast_to(column, (INST, LANES)), 0.0)
        return jnp.broadcast_to(jnp.sum(spread, axis=0, keepdims=True), (8, LANES))

    def to_column(row):
        spread = jnp.where(diagonal, jnp.broadcast_to(row[0:1, :], (INST, LANES)), 0.0)
        return jnp.sum(spread, axis=1, keepdims=True)

    square = lax.broadcasted_iota(jnp.int32, (INST, INST), 1) == lax.broadcasted_iota(jnp.int32, (INST, INST), 0)

    def ratio(n):
        row = numer_ref[n : n + 1, :].astype(F32) / denom_ref[n : n + 1, :].astype(F32)
        return jnp.sum(jnp.where(square, jnp.broadcast_to(row, (INST, INST)), 0.0), axis=1, keepdims=True)

    def spread(column):
        return jnp.broadcast_to(column, (INST, LANES))

    def wait_all(copies):
        for c in copies:
            c.wait()

    def team_rows(which):
        return [
            remote(rows_t.at[which, yc], rows_t.at[which, yc], t_ss.at[which, k - 1], t_rs.at[which, k - 1], team_peer(k))
            for k in team_order
        ]

    def sum_team(which):
        total = rows_t[which, 0]
        for i in range(1, TEAM):
            total = total + rows_t[which, i]
        return total

    def far_row(which):
        return remote(rows_p.at[which], rows_pr.at[which], p_ss.at[which], p_rs.at[which], far_peer)

    def product(k):
        j = flip(x, k)
        out = jnp.dot(dbf_ref[...], m_ref[:, at(j, WIDE)], preferred_element_type=F32)
        for gz in range(SIDE):
            for part in range(CHUNK // LANES):
                start = gz * CHUNK + part * LANES
                own_ref[j, gz, part * INST : (part + 1) * INST] = out[:, start : start + LANES]
        if k:
            s1x[k - 1] = own_ref[j, :, :CUT].astype(BF16)
        for q in near_last:
            s1z[q - 1, j] = own_ref[j, flip(zl, q), CUT:].astype(BF16)

    def send_product(k):
        j = flip(x, k)
        sent_x = None
        if k:
            sent_x = remote(s1x.at[k - 1], r1x.at[k - 1], a_ss.at[0, k - 1], a_rs.at[0, k - 1], x_peer(k))
        sent_z = [
            remote(s1z.at[q - 1, j], r1z.at[q - 1, j], s_ss.at[q - 1, k], s_rs.at[q - 1, k], z_peer(q)) for q in near_last
        ]
        return sent_x, sent_z

    def scatter_dual():
        sends = {}
        for k in order:
            product(k)
            sends[k] = send_product(k)
        return sends

    def second_dual(sends):
        later = []

        def finish_z(k):
            j = flip(x, k)
            wait_all(sends[k][1])
            total = own_ref[j, zl, CUT:]
            for q in range(3):
                total = total + r1z[q, j].astype(F32)
            if k:
                s2x[k - 1] = total.astype(BF16)
                later.append(remote(s2x.at[k - 1], r2x.at[k - 1], a_ss.at[3, k - 1], a_rs.at[3, k - 1], x_peer(k)))
            else:
                t1_ref[...] = total

        finish_z(2)
        finish_z(1)
        for k in (1, 2, 3):
            sends[k][0].wait()
        t0_ref[...] = own_ref[x, :, :CUT] + r1x[0].astype(F32) + r1x[1].astype(F32) + r1x[2].astype(F32)
        for k in near_last:
            s2z[k - 1] = t0_ref[flip(zl, k)].astype(BF16)
            later.append(remote(s2z.at[k - 1], r2z.at[k - 1], a_ss.at[2, k - 1], a_rs.at[2, k - 1], z_peer(k)))
        finish_z(3)
        finish_z(0)
        return later

    def gather_dual(later, process, aside=None, before=None, process_far=None):
        wait_all(later)
        upper = t0_ref[zl] + r2z[0].astype(F32) + r2z[1].astype(F32) + r2z[2].astype(F32)
        lower = t1_ref[...] + r2x[0].astype(F32) + r2x[1].astype(F32) + r2x[2].astype(F32)
        gather[x, zl, :CUT] = upper.astype(BF16)
        gather[x, zl, CUT:] = lower.astype(BF16)
        above = pl.ds(0, CUT_OUT)
        below = pl.ds(CUT_OUT, STACK - CUT_OUT)
        mine_above = gather.at[x, zl, above]
        mine_below = gather.at[x, zl, below]
        z_own = {}
        x_own = {}
        z_more = {}
        x_more = {}
        for k in near_last:
            z_own[k] = remote(mine_above, mine_above, a_ss.at[4, k - 1], a_rs.at[4, k - 1], z_peer(k))
            x_own[k] = remote(mine_below, mine_below, a_ss.at[5, k - 1], a_rs.at[5, k - 1], x_peer(k))
        for k in near_last:
            z_more[k] = remote(mine_below, mine_below, a_ss.at[6, k - 1], a_rs.at[6, k - 1], z_peer(k))
            x_more[k] = remote(mine_above, mine_above, a_ss.at[7, k - 1], a_rs.at[7, k - 1], x_peer(k))
        if before is not None:
            before()
        process(x, zl)
        from_x = {}
        from_z = {}
        for k in (1, 3, 2):
            x_own[k].wait()
            part = gather.at[flip(x, k), zl, below]
            for q in near_last:
                from_z[k, q] = remote(part, part, f_ss.at[1, k - 1, q - 1], f_rs.at[1, k - 1, q - 1], z_peer(q))
            z_own[k].wait()
            part = gather.at[x, flip(zl, k), above]
            for q in near_last:
                from_x[q, k] = remote(part, part, f_ss.at[0, k - 1, q - 1], f_rs.at[0, k - 1, q - 1], x_peer(q))
        for k in (1, 3, 2):
            z_more[k].wait()
            process(x, flip(zl, k))
            x_more[k].wait()
            process(flip(x, k), zl)
        if aside is not None:
            aside()
        for qx, qz in far_pieces:
            from_x[qx, qz].wait()
            from_z[qx, qz].wait()
            (process_far or process)(flip(x, qx), flip(zl, qz))

    def halves(body):
        def process(gx, gz):
            for part in range(CHUNK // LANES):
                cols = at((gx * SIDE + gz) * (CHUNK // LANES) + part, LANES)
                image = gather[gx, gz, part * INST : (part + 1) * INST].astype(F32)
                body(image, cols)

        return process

    started = set()

    def with_product(body, rows, uses):
        done = halves(body)

        def process(gx, gz):
            done(gx, gz)
            cols = at(gx * SIDE + gz, CHUNK)
            out = lax.dot_general(
                e_ref[rows, cols], m_ref[:, cols], (((1,), (1,)), ((), ())), preferred_element_type=F32
            )
            for n, u in enumerate(uses):
                for i in range(TEAM):
                    part = out[n * INST : (n + 1) * INST, i * PIECE : (i + 1) * PIECE]
                    if u in started:
                        z_ref[u, i] += part
                    else:
                        z_ref[u, i] = part
            started.update(uses)

        return process

    def wide_image(u):
        for i in range(SIDE):
            out = lax.dot_general(
                e_ref[INST:, :], m_ref[i * 2 * PIECE : (i + 1) * 2 * PIECE, :], (((1,), (1,)), ((), ())),
                preferred_element_type=F32,
            )
            z_ref[u, 2 * i] = out[:, :PIECE]
            z_ref[u, 2 * i + 1] = out[:, PIECE:]

    def scatter_primal(u):
        sends = []
        for k in team_order:
            sb[u, k - 1] = z_ref[u, flip(yc, k)].astype(BF16)
            sends.append(remote(sb.at[u, k - 1], rb.at[u, k - 1], b_ss.at[u, k - 1], b_rs.at[u, k - 1], team_peer(k)))
        return sends

    def far_primal(u, sends):
        wait_all(sends)
        total = z_ref[u, yc]
        for k in range(1, TEAM):
            total = total + rb[u, k - 1].astype(F32)
        zs[u] = total.astype(BF16)
        return remote(zs.at[u], zr.at[u], z_ss.at[u], z_rs.at[u], far_peer)

    def done_primal(u, copy):
        copy.wait()
        return zs[u].astype(F32) + zr[u].astype(F32)

    def gather_primal(v):
        return [
            remote(gb.at[v, yc], gb.at[v, yc], g_ss.at[v, k - 1], g_rs.at[v, k - 1], team_peer(k)) for k in team_order
        ]

    def fill_dual(v):
        for i in range(TEAM):
            dbf_ref[:, i * PIECE : (i + 1) * PIECE] = gb[v, i]

    own_cols = at(yc, PIECE)

    load_d0.wait()
    dbf_ref[...] = d0_ref[...].astype(BF16)
    load_cp.wait()
    sum_ref[...] = jnp.zeros_like(sum_ref)

    def square_step(i, _):
        c = cp_ref[:, at(i, LANES)].astype(F32)
        sum_ref[...] += c * c
        return 0

    lax.fori_loop(0, COLS // LANES, square_step, 0, unroll=4)
    rows_t[0, yc] = to_row(jnp.sum(sum_ref[...], axis=1, keepdims=True))
    for position, k in enumerate(order):
        m_loads[position].wait()
        product(k)
    pl.semaphore_wait(barrier, 13 + border)

    @pl.when(border == 1)
    def _():
        pl.semaphore_signal(far_in, inc=1, device_id=across, device_id_type=MESH)

    sends = {k: send_product(k) for k in order}
    norm_copies = team_rows(0)

    wait_all(small_loads)
    load_ct.wait()
    code = code_ref[...]
    half_code = code // 2
    low_ref[...] = -0.25 - 0.75 * (code - 2 * half_code).astype(F32)
    high_ref[...] = 0.25 + 0.75 * half_code.astype(F32)
    theta_ref[...] = spread(ratio(2))

    @pl.when(border == 1)
    def _():
        pl.semaphore_wait(far_in, 1)
        pl.semaphore_signal(far_in, inc=1, device_id=z_peer(1), device_id_type=MESH)

    wait_all(norm_copies)
    rows_p[0] = sum_team(0)
    later = second_dual(sends)

    @pl.when(border == 0)
    def _():
        pl.semaphore_wait(far_in, 1)

    norm_far = far_row(0)

    def steps_of_scale():
        norm_far.wait()
        norm_sum = to_column(rows_p[0] + rows_pr[0])
        scale = jnp.sqrt(norm_sum / VARS + EPS)
        tau_ref[...] = spread(ratio(0) / scale)
        sigma_ref[...] = spread(ratio(1) * scale)
        scale2_ref[...] = spread(VARS * scale * scale)

    def first_step(image, cols):
        reduced = cp_ref[:, cols].astype(F32) - image
        shifted = 0.0 - tau_ref[...] * reduced
        projected = jnp.minimum(jnp.maximum(shifted, low_ref[:, cols]), high_ref[:, cols])
        red0_ref[:, cols] = reduced
        sh0_ref[:, cols] = shifted
        e_ref[:INST, cols] = (projected + theta_ref[...] * projected).astype(BF16)

    gather_dual(later, with_product(first_step, slice(0, INST), (0,)), before=steps_of_scale)

    sends = scatter_primal(0)

    def slope_of(shifted, cols):
        return jax.nn.sigmoid(SHARP * (shifted - low_ref[:, cols])) * jax.nn.sigmoid(
            SHARP * (high_ref[:, cols] - shifted)
        )

    far = far_primal(0, sends)
    image = done_primal(0, far)
    residue0 = right_ref[:, own_cols] - image
    dual1 = d0_ref[:, own_cols] + sigma_ref[...] * residue0
    gb[0, yc] = dual1.astype(BF16)
    gathers = gather_primal(0)
    dual1_ref[...] = dual1
    weigh_ref[...] = sigma_ref[...] * residue0
    wait_all(gathers)
    fill_dual(0)

    sends = scatter_dual()
    def slope_step(i, _):
        cols = at(i, LANES)
        slope = slope_of(sh0_ref[:, cols], cols)
        slope0_ref[:, cols] = slope
        e_ref[INST:, cols] = (slope * red0_ref[:, cols]).astype(BF16)
        return 0

    lax.fori_loop(0, COLS // LANES, slope_step, 0, unroll=2)
    wide_image(1)
    weigh_sends = scatter_primal(1)
    later = second_dual(sends)

    def second_step(image, cols):
        low, high = low_ref[:, cols], high_ref[:, cols]
        reduced = cp_ref[:, cols].astype(F32) - image
        before = jnp.minimum(jnp.maximum(sh0_ref[:, cols], low), high)
        shifted = before - tau_ref[...] * reduced
        primal_ref[:, cols] = shifted
        grad_ref[:, cols] = reduced
        slope_adj = slope_of(shifted, cols) * ct_ref[:, cols].astype(F32)
        sa1_ref[:, cols] = slope_adj
        e_ref[:INST, cols] = (tau_ref[...] * slope_adj).astype(BF16)

    def primal_step(image, cols):
        low, high = low_ref[:, cols], high_ref[:, cols]
        before = jnp.minimum(jnp.maximum(sh0_ref[:, cols], low), high)
        projected = jnp.minimum(jnp.maximum(primal_ref[:, cols], low), high)
        primal_ref[:, cols] = projected
        e_ref[INST:, cols] = (projected + theta_ref[...] * (projected - before)).astype(BF16)
        slope_adj = sa1_ref[:, cols]
        sum_ref[...] += slope_adj * grad_ref[:, cols] + slope_adj * (slope0_ref[:, cols] * red0_ref[:, cols])

    def both_steps(image, cols):
        second_step(image, cols)
        primal_step(image, cols)

    sum_ref[...] = jnp.zeros_like(sum_ref)
    gather_dual(
        later,
        with_product(both_steps, slice(0, 2 * INST), (2, 3)),
        process_far=with_product(second_step, slice(0, INST), (2,)),
    )

    sends = scatter_primal(2)
    weigh_far = far_primal(1, weigh_sends)
    primal_process = with_product(primal_step, slice(INST, 2 * INST), (3,))
    for qx, qz in far_pieces:
        primal_process(flip(x, qx), flip(zl, qz))
    primal_copy = pltpu.make_async_copy(primal_ref, primal_out, out_sem.at[0])
    primal_copy.start()
    rows_t[1, yc] = to_row(tau_ref[:, 0:1] * jnp.sum(sum_ref[...], axis=1, keepdims=True))
    far = far_primal(2, sends)
    end_sends = scatter_primal(3)
    factor_copies = team_rows(1)
    adjoint = done_primal(2, far)
    rounded = adjoint.astype(BF16)
    gb[1, yc] = rounded
    gathers = gather_primal(1)
    wimg_ref[...] = tau_ref[...] * (1.0 + theta_ref[...]) * sigma_ref[...] * done_primal(1, weigh_far)
    weighed = adjoint * weigh_ref[...] - rounded.astype(F32) * wimg_ref[...]
    rows_t[2, yc] = to_row(jnp.sum(weighed, axis=1, keepdims=True))
    wait_all(factor_copies)
    factor_copies = team_rows(2)
    rows_p[1] = sum_team(1)
    factor_far = far_row(1)
    wait_all(gathers)
    fill_dual(1)

    sends = scatter_dual()
    end_far = far_primal(3, end_sends)
    wait_all(factor_copies)
    rowx[x] = sum_team(2)
    x_rows = [remote(rowx.at[x], rowx.at[x], rx_ss.at[k - 1], rx_rs.at[k - 1], x_peer(k)) for k in (1, 2, 3)]
    later = second_dual(sends)
    wait_all(x_rows)
    rowz[zl] = rowx[0] + rowx[1] + rowx[2] + rowx[3]
    z_rows = [remote(rowz.at[zl], rowz.at[zl], rz_ss.at[k - 1], rz_rs.at[k - 1], z_peer(k)) for k in (1, 2, 3)]
    factor_far.wait()
    residue1 = right_ref[:, own_cols] - done_primal(3, end_far)
    gd[yc] = dual1_ref[...] + sigma_ref[...] * residue1
    dual_gathers = [
        remote(gd.at[yc], gd.at[yc], gd_ss.at[k - 1], gd_rs.at[k - 1], team_peer(k)) for k in team_order
    ]
    wait_all(z_rows)
    factors = to_column(rows_p[1] + rows_pr[1] + (rowz[0] + rowz[1] + rowz[2] + rowz[3]))
    sum_ref[...] = spread(factors) / scale2_ref[...]

    def last_step(image, cols):
        slope_adj = sa1_ref[:, cols]
        ahead = slope_adj - (1.0 + theta_ref[...]) * (sigma_ref[...] * image)
        gradient = tau_ref[...] * (slope_adj + slope0_ref[:, cols] * ahead)
        grad_ref[:, cols] = cp_ref[:, cols].astype(F32) * sum_ref[...] - gradient

    grad_process = halves(last_step)
    out_copies = []

    def process(gx, gz):
        grad_process(gx, gz)
        cols = at(gx * SIDE + gz, CHUNK)
        copy = pltpu.make_async_copy(grad_ref.at[:, cols], grad_out.at[:, cols], out_sem.at[2 + len(out_copies)])
        copy.start()
        out_copies.append(copy)

    dual_copy = pltpu.make_async_copy(dual_ref, dual_out, out_sem.at[1])

    def dual_end():
        wait_all(dual_gathers)
        for i in range(TEAM):
            dual_ref[:, i * PIECE : (i + 1) * PIECE] = gd[i]
        dual_copy.start()

    gather_dual(later, process, dual_end)
    primal_copy.wait()
    dual_copy.wait()
    wait_all(out_copies)


def keep(a, b, c, out_a, out_b, out_c, hold_a, hold_b, hold_c, in_sem, out_sem):
    ways = [(b, hold_b, out_b)]
    for n in range(4):
        rows = pl.ds(n * 16, 16)
        ways.append((a.at[rows], hold_a.at[rows], out_a.at[rows]))
        ways.append((c.at[rows], hold_c.at[rows], out_c.at[rows]))
    loads = [pltpu.make_async_copy(src, hold, in_sem.at[n]) for n, (src, hold, _) in enumerate(ways)]
    stores = [pltpu.make_async_copy(hold, dst, out_sem.at[n]) for n, (_, hold, dst) in enumerate(ways)]
    for copy in loads:
        copy.start()
    for load, store in zip(loads, stores):
        load.wait()
        store.start()
    for copy in stores:
        copy.wait()


def local(matrix, cost_pred, cost_true, dual_start, right_side, bound_code, step_numer, step_denom):
    dma = pltpu.SemaphoreType.DMA
    v = pltpu.VMEM
    anywhere = pl.BlockSpec(memory_space=pl.ANY)
    uses, rows = 4, 3
    scratch = [
        v((INST, COLS), F32), v((INST, ROWS), F32), v((INST, COLS), F32), dma((2 + SIDE * SIDE,)),
        v((ROWS, COLS), BF16), dma((SIDE,)), v((INST, COLS), BF16), v((INST, COLS), BF16), v((INST, ROWS), F32),
        v((1, ROWS), F32), v((1, COLS), jnp.int32), v((3, INST), jnp.int32), v((3, INST), jnp.int32), dma((7,)),
        v((INST, LANES), F32), v((INST, LANES), F32), v((INST, LANES), F32), v((INST, LANES), F32),
        v((1, COLS), F32), v((1, COLS), F32), v((INST, LANES), F32),
        v((INST, ROWS), BF16), v((SIDE, SIDE, STACK, LANES), F32), v((SIDE, CUT, LANES), F32), v((REST, LANES), F32),
        v((INST, COLS), F32), v((INST, COLS), F32), v((INST, COLS), F32),
        v((INST, COLS), F32), v((2 * INST, COLS), BF16), v((uses, TEAM, INST, PIECE), F32),
        v((3, SIDE, CUT, LANES), BF16), v((3, SIDE, REST, LANES), BF16), v((3, SIDE, CUT, LANES), BF16),
        v((3, SIDE, REST, LANES), BF16), v((3, CUT, LANES), BF16), v((3, REST, LANES), BF16), v((3, CUT, LANES), BF16),
        v((3, REST, LANES), BF16), v((SIDE, SIDE, STACK, LANES), BF16),
        dma((8, 3)), dma((8, 3)), dma((3, SIDE)), dma((3, SIDE)), dma((2, 3, 3)), dma((2, 3, 3)),
        v((uses, TEAM - 1, INST, PIECE), BF16), v((uses, TEAM - 1, INST, PIECE), BF16),
        v((uses, INST, PIECE), BF16), v((uses, INST, PIECE), BF16),
        v((2, TEAM, INST, PIECE), BF16), v((TEAM, INST, PIECE), F32),
        dma((uses, TEAM - 1)), dma((uses, TEAM - 1)), dma((uses,)), dma((uses,)),
        dma((2, TEAM - 1)), dma((2, TEAM - 1)), dma((TEAM - 1,)), dma((TEAM - 1,)),
        v((rows, TEAM, 8, LANES), F32), v((2, 8, LANES), F32), v((2, 8, LANES), F32), v((SIDE, 8, LANES), F32),
        v((SIDE, 8, LANES), F32),
        dma((rows, TEAM - 1)), dma((rows, TEAM - 1)), dma((2,)), dma((2,)), dma((3,)), dma((3,)), dma((3,)), dma((3,)),
        v((INST, PIECE), F32), v((INST, PIECE), F32), v((INST, PIECE), F32), pltpu.SemaphoreType.REGULAR,
    ]
    outs = (
        jax.ShapeDtypeStruct((INST, COLS), F32),
        jax.ShapeDtypeStruct((INST, ROWS), F32),
        jax.ShapeDtypeStruct((INST, COLS), F32),
    )
    results = pl.pallas_call(
        kernel,
        out_shape=outs,
        in_specs=[anywhere] * 8,
        out_specs=(anywhere,) * 3,
        scratch_shapes=scratch,
        compiler_params=pltpu.CompilerParams(
            collective_id=0, has_side_effects=True, vmem_limit_bytes=63 * 2**20
        ),
    )(
        matrix,
        cost_pred,
        cost_true,
        dual_start,
        right_side.reshape(1, ROWS),
        bound_code.reshape(1, COLS),
        step_numer.T,
        step_denom.T,
    )
    return pl.pallas_call(
        keep,
        out_shape=outs,
        in_specs=[anywhere] * 3,
        out_specs=(anywhere,) * 3,
        scratch_shapes=[v((INST, COLS), F32), v((INST, ROWS), F32), v((INST, COLS), F32), dma((9,)), dma((9,))],
        compiler_params=pltpu.CompilerParams(vmem_limit_bytes=63 * 2**20),
    )(*results)


def solution(mesh):
    placed = (
        P("rows", "cols"),
        P(None, "cols"),
        P(None, "cols"),
        P(None, "rows"),
        P("rows"),
        P("cols"),
        P(),
        P(),
    )
    return jax.shard_map(
        local,
        mesh=mesh,
        in_specs=placed,
        out_specs=(P(None, "cols"), P(None, "rows"), P(None, "cols")),
        check_vma=False,
    )
```

```python
import jax
import jax.numpy as jnp
from jax import lax
from jax.experimental import pallas as pl
from jax.experimental.pallas import tpu as pltpu
from jax.sharding import PartitionSpec as P

VARS = 65536
MESH = pl.DeviceIdType.MESH
F32 = jnp.float32
BF16 = jnp.bfloat16
SHARP = 16.0
EPS = 1e-06

INST = 64
CUT = 80
ROWS = 1024
COLS = 4096
SIDE = 4
WIDE = COLS // SIDE
CHUNK = WIDE // SIDE
TEAM = 8
PIECE = ROWS // TEAM
LANES = 128
CUT_OUT = 96
STACK = INST * CHUNK // LANES
REST = STACK - CUT


def kernel(
    m_hbm, cp_hbm, ct_hbm, d0_hbm, right_hbm, code_hbm, numer_hbm, denom_hbm,
    primal_ref, dual_ref, grad_ref,
    m_ref, m_sem, cp_ref, ct_ref, d0_ref, right_ref, code_ref, numer_ref, denom_ref, in_sem,
    tau_ref, sigma_ref, theta_ref, scale2_ref, low_ref, high_ref, sum_ref,
    dbf_ref, own_ref, t0_ref, t1_ref, red0_ref, sh0_ref, slope0_ref, sa1_ref, e_ref, z_ref,
    s1x, s1z, r1x, r1z, s2z, s2x, r2z, r2x, gather,
    a_ss, a_rs, s_ss, s_rs, f_ss, f_rs,
    sb, rb, zs, zr, gb, gd,
    b_ss, b_rs, z_ss, z_rs, g_ss, g_rs, gd_ss, gd_rs,
    rows_t, rows_p, rows_pr, rowx, rowz,
    t_ss, t_rs, p_ss, p_rs, rx_ss, rx_rs, rz_ss, rz_rs,
    dual1_ref, weigh_ref, wimg_ref, far_in,
):
    rr = lax.axis_index("rows")
    cc = lax.axis_index("cols")
    x, zl = rr // SIDE, lax.rem(rr, SIDE)
    zh, yc = cc // TEAM, lax.rem(cc, TEAM)
    y = yc // 2

    def flip(value, k):
        if k == 0:
            return value
        total = value
        for bit in (1, 2, 4):
            if k & bit:
                total = total + bit - 2 * bit * lax.rem(value // bit, 2)
        return total

    def x_peer(k):
        return (flip(x, k) * SIDE + zl, cc)

    def z_peer(k):
        return (x * SIDE + flip(zl, k), cc)

    def team_peer(k):
        return (rr, zh * TEAM + flip(yc, k))

    far_peer = (rr, (1 - zh) * TEAM + yc)

    def remote(src, dst, send, recv, peer):
        copy = pltpu.make_async_remote_copy(
            src_ref=src, dst_ref=dst, send_sem=send, recv_sem=recv, device_id=peer, device_id_type=MESH
        )
        copy.start()
        return copy

    def at(value, size):
        return pl.ds(pl.multiple_of(value * size, size), size)

    order = (2, 1, 3, 0)
    near_last = (2, 3, 1)
    far_pieces = ((1, 1), (3, 1), (1, 3), (3, 3), (2, 1), (1, 2), (2, 3), (3, 2), (2, 2))
    team_order = (4, 5, 6, 7, 2, 3, 1)

    def load(n, src, dst):
        copy = pltpu.make_async_copy(src, dst, in_sem.at[n])
        copy.start()
        return copy

    load_d0 = load(0, d0_hbm, d0_ref)
    load_cp = load(1, cp_hbm, cp_ref)
    m_loads = []
    for k in order:
        cols = at(flip(x, k), WIDE)
        copy = pltpu.make_async_copy(m_hbm.at[:, cols], m_ref.at[:, cols], m_sem.at[k])
        copy.start()
        m_loads.append(copy)
    small_loads = [
        load(2, right_hbm, right_ref), load(3, code_hbm, code_ref),
        load(4, numer_hbm, numer_ref), load(5, denom_hbm, denom_ref),
    ]
    load_ct = load(6, ct_hbm, ct_ref)

    barrier = pltpu.get_barrier_semaphore()
    for k in (1, 2, 3):
        pl.semaphore_signal(barrier, inc=1, device_id=x_peer(k), device_id_type=MESH)
        pl.semaphore_signal(barrier, inc=1, device_id=z_peer(k), device_id_type=MESH)
    for k in range(1, TEAM):
        pl.semaphore_signal(barrier, inc=1, device_id=team_peer(k), device_id_type=MESH)

    border = 1 - lax.rem((zl + 1) // 2, 2)
    across = (x * SIDE + (SIDE - 1 - zl), (1 - zh) * TEAM + yc)

    @pl.when(border == 1)
    def _():
        pl.semaphore_signal(barrier, inc=1, device_id=across, device_id_type=MESH)


    lane = lax.broadcasted_iota(jnp.int32, (INST, LANES), 1)
    diagonal = lane == lax.broadcasted_iota(jnp.int32, (INST, LANES), 0)

    def to_row(column):
        spread = jnp.where(diagonal, jnp.broadcast_to(column, (INST, LANES)), 0.0)
        return jnp.broadcast_to(jnp.sum(spread, axis=0, keepdims=True), (8, LANES))

    def to_column(row):
        spread = jnp.where(diagonal, jnp.broadcast_to(row[0:1, :], (INST, LANES)), 0.0)
        return jnp.sum(spread, axis=1, keepdims=True)

    square = lax.broadcasted_iota(jnp.int32, (INST, INST), 1) == lax.broadcasted_iota(jnp.int32, (INST, INST), 0)

    def ratio(n):
        row = numer_ref[n : n + 1, :].astype(F32) / denom_ref[n : n + 1, :].astype(F32)
        return jnp.sum(jnp.where(square, jnp.broadcast_to(row, (INST, INST)), 0.0), axis=1, keepdims=True)

    def spread(column):
        return jnp.broadcast_to(column, (INST, LANES))

    def wait_all(copies):
        for c in copies:
            c.wait()

    def team_rows(which):
        return [
            remote(rows_t.at[which, yc], rows_t.at[which, yc], t_ss.at[which, k - 1], t_rs.at[which, k - 1], team_peer(k))
            for k in team_order
        ]

    def sum_team(which):
        total = rows_t[which, 0]
        for i in range(1, TEAM):
            total = total + rows_t[which, i]
        return total

    def far_row(which):
        return remote(rows_p.at[which], rows_pr.at[which], p_ss.at[which], p_rs.at[which], far_peer)

    def product(k):
        j = flip(x, k)
        out = jnp.dot(dbf_ref[...], m_ref[:, at(j, WIDE)], preferred_element_type=F32)
        for gz in range(SIDE):
            for part in range(CHUNK // LANES):
                start = gz * CHUNK + part * LANES
                own_ref[j, gz, part * INST : (part + 1) * INST] = out[:, start : start + LANES]
        if k:
            s1x[k - 1] = own_ref[j, :, :CUT].astype(BF16)
        for q in near_last:
            s1z[q - 1, j] = own_ref[j, flip(zl, q), CUT:].astype(BF16)

    def send_product(k):
        j = flip(x, k)
        sent_x = None
        if k:
            sent_x = remote(s1x.at[k - 1], r1x.at[k - 1], a_ss.at[0, k - 1], a_rs.at[0, k - 1], x_peer(k))
        sent_z = [
            remote(s1z.at[q - 1, j], r1z.at[q - 1, j], s_ss.at[q - 1, k], s_rs.at[q - 1, k], z_peer(q)) for q in near_last
        ]
        return sent_x, sent_z

    def scatter_dual():
        sends = {}
        for k in order:
            product(k)
            sends[k] = send_product(k)
        return sends

    def second_dual(sends):
        later = []

        def finish_z(k):
            j = flip(x, k)
            wait_all(sends[k][1])
            total = own_ref[j, zl, CUT:]
            for q in range(3):
                total = total + r1z[q, j].astype(F32)
            if k:
                s2x[k - 1] = total.astype(BF16)
                later.append(remote(s2x.at[k - 1], r2x.at[k - 1], a_ss.at[3, k - 1], a_rs.at[3, k - 1], x_peer(k)))
            else:
                t1_ref[...] = total

        finish_z(2)
        finish_z(1)
        for k in (1, 2, 3):
            sends[k][0].wait()
        t0_ref[...] = own_ref[x, :, :CUT] + r1x[0].astype(F32) + r1x[1].astype(F32) + r1x[2].astype(F32)
        for k in near_last:
            s2z[k - 1] = t0_ref[flip(zl, k)].astype(BF16)
            later.append(remote(s2z.at[k - 1], r2z.at[k - 1], a_ss.at[2, k - 1], a_rs.at[2, k - 1], z_peer(k)))
        finish_z(3)
        finish_z(0)
        return later

    def gather_dual(later, process, aside=None, before=None, process_far=None):
        wait_all(later)
        upper = t0_ref[zl] + r2z[0].astype(F32) + r2z[1].astype(F32) + r2z[2].astype(F32)
        lower = t1_ref[...] + r2x[0].astype(F32) + r2x[1].astype(F32) + r2x[2].astype(F32)
        gather[x, zl, :CUT] = upper.astype(BF16)
        gather[x, zl, CUT:] = lower.astype(BF16)
        above = pl.ds(0, CUT_OUT)
        below = pl.ds(CUT_OUT, STACK - CUT_OUT)
        mine_above = gather.at[x, zl, above]
        mine_below = gather.at[x, zl, below]
        z_own = {}
        x_own = {}
        z_more = {}
        x_more = {}
        for k in near_last:
            z_own[k] = remote(mine_above, mine_above, a_ss.at[4, k - 1], a_rs.at[4, k - 1], z_peer(k))
            x_own[k] = remote(mine_below, mine_below, a_ss.at[5, k - 1], a_rs.at[5, k - 1], x_peer(k))
        for k in near_last:
            z_more[k] = remote(mine_below, mine_below, a_ss.at[6, k - 1], a_rs.at[6, k - 1], z_peer(k))
            x_more[k] = remote(mine_above, mine_above, a_ss.at[7, k - 1], a_rs.at[7, k - 1], x_peer(k))
        if before is not None:
            before()
        process(x, zl)
        from_x = {}
        from_z = {}
        for k in (1, 3, 2):
            x_own[k].wait()
            part = gather.at[flip(x, k), zl, below]
            for q in near_last:
                from_z[k, q] = remote(part, part, f_ss.at[1, k - 1, q - 1], f_rs.at[1, k - 1, q - 1], z_peer(q))
            z_own[k].wait()
            part = gather.at[x, flip(zl, k), above]
            for q in near_last:
                from_x[q, k] = remote(part, part, f_ss.at[0, k - 1, q - 1], f_rs.at[0, k - 1, q - 1], x_peer(q))
        for k in (1, 3, 2):
            z_more[k].wait()
            process(x, flip(zl, k))
            x_more[k].wait()
            process(flip(x, k), zl)
        if aside is not None:
            aside()
        for qx, qz in far_pieces:
            from_x[qx, qz].wait()
            from_z[qx, qz].wait()
            (process_far or process)(flip(x, qx), flip(zl, qz))

    def halves(body):
        def process(gx, gz):
            for part in range(CHUNK // LANES):
                cols = at((gx * SIDE + gz) * (CHUNK // LANES) + part, LANES)
                image = gather[gx, gz, part * INST : (part + 1) * INST].astype(F32)
                body(image, cols)

        return process

    started = set()

    def with_product(body, rows, uses):
        done = halves(body)

        def process(gx, gz):
            done(gx, gz)
            cols = at(gx * SIDE + gz, CHUNK)
            out = lax.dot_general(
                e_ref[rows, cols], m_ref[:, cols], (((1,), (1,)), ((), ())), preferred_element_type=F32
            )
            for n, u in enumerate(uses):
                for i in range(TEAM):
                    part = out[n * INST : (n + 1) * INST, i * PIECE : (i + 1) * PIECE]
                    if u in started:
                        z_ref[u, i] += part
                    else:
                        z_ref[u, i] = part
            started.update(uses)

        return process

    def wide_image(u):
        for i in range(SIDE):
            out = lax.dot_general(
                e_ref[INST:, :], m_ref[i * 2 * PIECE : (i + 1) * 2 * PIECE, :], (((1,), (1,)), ((), ())),
                preferred_element_type=F32,
            )
            z_ref[u, 2 * i] = out[:, :PIECE]
            z_ref[u, 2 * i + 1] = out[:, PIECE:]

    def scatter_primal(u):
        sends = []
        for k in team_order:
            sb[u, k - 1] = z_ref[u, flip(yc, k)].astype(BF16)
            sends.append(remote(sb.at[u, k - 1], rb.at[u, k - 1], b_ss.at[u, k - 1], b_rs.at[u, k - 1], team_peer(k)))
        return sends

    def far_primal(u, sends):
        wait_all(sends)
        total = z_ref[u, yc]
        for k in range(1, TEAM):
            total = total + rb[u, k - 1].astype(F32)
        zs[u] = total.astype(BF16)
        return remote(zs.at[u], zr.at[u], z_ss.at[u], z_rs.at[u], far_peer)

    def done_primal(u, copy):
        copy.wait()
        return zs[u].astype(F32) + zr[u].astype(F32)

    def gather_primal(v):
        return [
            remote(gb.at[v, yc], gb.at[v, yc], g_ss.at[v, k - 1], g_rs.at[v, k - 1], team_peer(k)) for k in team_order
        ]

    def fill_dual(v):
        for i in range(TEAM):
            dbf_ref[:, i * PIECE : (i + 1) * PIECE] = gb[v, i]

    own_cols = at(yc, PIECE)

    load_d0.wait()
    dbf_ref[...] = d0_ref[...].astype(BF16)
    load_cp.wait()
    sum_ref[...] = jnp.zeros_like(sum_ref)

    def square_step(i, _):
        c = cp_ref[:, at(i, LANES)].astype(F32)
        sum_ref[...] += c * c
        return 0

    lax.fori_loop(0, COLS // LANES, square_step, 0, unroll=4)
    rows_t[0, yc] = to_row(jnp.sum(sum_ref[...], axis=1, keepdims=True))
    for position, k in enumerate(order):
        m_loads[position].wait()
        product(k)
    pl.semaphore_wait(barrier, 13 + border)

    @pl.when(border == 1)
    def _():
        pl.semaphore_signal(far_in, inc=1, device_id=across, device_id_type=MESH)

    sends = {k: send_product(k) for k in order}
    norm_copies = team_rows(0)

    wait_all(small_loads)
    load_ct.wait()
    code = code_ref[...]
    half_code = code // 2
    low_ref[...] = -0.25 - 0.75 * (code - 2 * half_code).astype(F32)
    high_ref[...] = 0.25 + 0.75 * half_code.astype(F32)
    theta_ref[...] = spread(ratio(2))

    @pl.when(border == 1)
    def _():
        pl.semaphore_wait(far_in, 1)
        pl.semaphore_signal(far_in, inc=1, device_id=z_peer(1), device_id_type=MESH)

    wait_all(norm_copies)
    rows_p[0] = sum_team(0)
    later = second_dual(sends)

    @pl.when(border == 0)
    def _():
        pl.semaphore_wait(far_in, 1)

    norm_far = far_row(0)

    def steps_of_scale():
        norm_far.wait()
        norm_sum = to_column(rows_p[0] + rows_pr[0])
        scale = jnp.sqrt(norm_sum / VARS + EPS)
        tau_ref[...] = spread(ratio(0) / scale)
        sigma_ref[...] = spread(ratio(1) * scale)
        scale2_ref[...] = spread(VARS * scale * scale)

    def first_step(image, cols):
        reduced = cp_ref[:, cols].astype(F32) - image
        shifted = 0.0 - tau_ref[...] * reduced
        projected = jnp.minimum(jnp.maximum(shifted, low_ref[:, cols]), high_ref[:, cols])
        red0_ref[:, cols] = reduced
        sh0_ref[:, cols] = shifted
        e_ref[:INST, cols] = (projected + theta_ref[...] * projected).astype(BF16)

    gather_dual(later, with_product(first_step, slice(0, INST), (0,)), before=steps_of_scale)

    sends = scatter_primal(0)

    def slope_of(shifted, cols):
        return jax.nn.sigmoid(SHARP * (shifted - low_ref[:, cols])) * jax.nn.sigmoid(
            SHARP * (high_ref[:, cols] - shifted)
        )

    far = far_primal(0, sends)
    image = done_primal(0, far)
    residue0 = right_ref[:, own_cols] - image
    dual1 = d0_ref[:, own_cols] + sigma_ref[...] * residue0
    gb[0, yc] = dual1.astype(BF16)
    gathers = gather_primal(0)
    dual1_ref[...] = dual1
    weigh_ref[...] = sigma_ref[...] * residue0
    wait_all(gathers)
    fill_dual(0)

    sends = scatter_dual()
    def slope_step(i, _):
        cols = at(i, LANES)
        slope = slope_of(sh0_ref[:, cols], cols)
        slope0_ref[:, cols] = slope
        e_ref[INST:, cols] = (slope * red0_ref[:, cols]).astype(BF16)
        return 0

    lax.fori_loop(0, COLS // LANES, slope_step, 0, unroll=2)
    wide_image(1)
    weigh_sends = scatter_primal(1)
    later = second_dual(sends)

    def second_step(image, cols):
        low, high = low_ref[:, cols], high_ref[:, cols]
        reduced = cp_ref[:, cols].astype(F32) - image
        before = jnp.minimum(jnp.maximum(sh0_ref[:, cols], low), high)
        shifted = before - tau_ref[...] * reduced
        primal_ref[:, cols] = shifted
        grad_ref[:, cols] = reduced
        slope_adj = slope_of(shifted, cols) * ct_ref[:, cols].astype(F32)
        sa1_ref[:, cols] = slope_adj
        e_ref[:INST, cols] = (tau_ref[...] * slope_adj).astype(BF16)

    def primal_step(image, cols):
        low, high = low_ref[:, cols], high_ref[:, cols]
        before = jnp.minimum(jnp.maximum(sh0_ref[:, cols], low), high)
        projected = jnp.minimum(jnp.maximum(primal_ref[:, cols], low), high)
        primal_ref[:, cols] = projected
        e_ref[INST:, cols] = (projected + theta_ref[...] * (projected - before)).astype(BF16)
        slope_adj = sa1_ref[:, cols]
        sum_ref[...] += slope_adj * grad_ref[:, cols] + slope_adj * (slope0_ref[:, cols] * red0_ref[:, cols])

    def both_steps(image, cols):
        second_step(image, cols)
        primal_step(image, cols)

    sum_ref[...] = jnp.zeros_like(sum_ref)
    gather_dual(
        later,
        with_product(both_steps, slice(0, 2 * INST), (2, 3)),
        process_far=with_product(second_step, slice(0, INST), (2,)),
    )

    sends = scatter_primal(2)
    weigh_far = far_primal(1, weigh_sends)
    primal_process = with_product(primal_step, slice(INST, 2 * INST), (3,))
    for qx, qz in far_pieces:
        primal_process(flip(x, qx), flip(zl, qz))
    rows_t[1, yc] = to_row(tau_ref[:, 0:1] * jnp.sum(sum_ref[...], axis=1, keepdims=True))
    far = far_primal(2, sends)
    end_sends = scatter_primal(3)
    factor_copies = team_rows(1)
    adjoint = done_primal(2, far)
    rounded = adjoint.astype(BF16)
    gb[1, yc] = rounded
    gathers = gather_primal(1)
    wimg_ref[...] = tau_ref[...] * (1.0 + theta_ref[...]) * sigma_ref[...] * done_primal(1, weigh_far)
    weighed = adjoint * weigh_ref[...] - rounded.astype(F32) * wimg_ref[...]
    rows_t[2, yc] = to_row(jnp.sum(weighed, axis=1, keepdims=True))
    wait_all(factor_copies)
    factor_copies = team_rows(2)
    rows_p[1] = sum_team(1)
    factor_far = far_row(1)
    wait_all(gathers)
    fill_dual(1)

    sends = scatter_dual()
    end_far = far_primal(3, end_sends)
    wait_all(factor_copies)
    rowx[x] = sum_team(2)
    x_rows = [remote(rowx.at[x], rowx.at[x], rx_ss.at[k - 1], rx_rs.at[k - 1], x_peer(k)) for k in (1, 2, 3)]
    later = second_dual(sends)
    wait_all(x_rows)
    rowz[zl] = rowx[0] + rowx[1] + rowx[2] + rowx[3]
    z_rows = [remote(rowz.at[zl], rowz.at[zl], rz_ss.at[k - 1], rz_rs.at[k - 1], z_peer(k)) for k in (1, 2, 3)]
    factor_far.wait()
    residue1 = right_ref[:, own_cols] - done_primal(3, end_far)
    gd[yc] = dual1_ref[...] + sigma_ref[...] * residue1
    dual_gathers = [
        remote(gd.at[yc], gd.at[yc], gd_ss.at[k - 1], gd_rs.at[k - 1], team_peer(k)) for k in team_order
    ]
    wait_all(z_rows)
    factors = to_column(rows_p[1] + rows_pr[1] + (rowz[0] + rowz[1] + rowz[2] + rowz[3]))
    sum_ref[...] = spread(factors) / scale2_ref[...]

    def last_step(image, cols):
        slope_adj = sa1_ref[:, cols]
        ahead = slope_adj - (1.0 + theta_ref[...]) * (sigma_ref[...] * image)
        gradient = tau_ref[...] * (slope_adj + slope0_ref[:, cols] * ahead)
        grad_ref[:, cols] = cp_ref[:, cols].astype(F32) * sum_ref[...] - gradient

    def dual_end():
        wait_all(dual_gathers)
        for i in range(TEAM):
            dual_ref[:, i * PIECE : (i + 1) * PIECE] = gd[i]

    gather_dual(later, halves(last_step), dual_end)


def keep(a, b, c, out_a, out_b, out_c, sem):
    ways = [(b, out_b)]
    for n in range(4):
        rows = pl.ds(n * 16, 16)
        ways.append((a.at[rows], out_a.at[rows]))
        ways.append((c.at[rows], out_c.at[rows]))
    stores = [pltpu.make_async_copy(src, dst, sem.at[n]) for n, (src, dst) in enumerate(ways)]
    for copy in stores:
        copy.start()
    for copy in stores:
        copy.wait()


def local(matrix, cost_pred, cost_true, dual_start, right_side, bound_code, step_numer, step_denom):
    dma = pltpu.SemaphoreType.DMA
    v = pltpu.VMEM
    anywhere = pl.BlockSpec(memory_space=pl.ANY)
    whole = pl.BlockSpec(memory_space=pltpu.VMEM)
    uses, rows = 4, 3
    scratch = [
        v((ROWS, COLS), BF16), dma((SIDE,)), v((INST, COLS), BF16), v((INST, COLS), BF16), v((INST, ROWS), F32),
        v((1, ROWS), F32), v((1, COLS), jnp.int32), v((3, INST), jnp.int32), v((3, INST), jnp.int32), dma((7,)),
        v((INST, LANES), F32), v((INST, LANES), F32), v((INST, LANES), F32), v((INST, LANES), F32),
        v((1, COLS), F32), v((1, COLS), F32), v((INST, LANES), F32),
        v((INST, ROWS), BF16), v((SIDE, SIDE, STACK, LANES), F32), v((SIDE, CUT, LANES), F32), v((REST, LANES), F32),
        v((INST, COLS), F32), v((INST, COLS), F32), v((INST, COLS), F32),
        v((INST, COLS), F32), v((2 * INST, COLS), BF16), v((uses, TEAM, INST, PIECE), F32),
        v((3, SIDE, CUT, LANES), BF16), v((3, SIDE, REST, LANES), BF16), v((3, SIDE, CUT, LANES), BF16),
        v((3, SIDE, REST, LANES), BF16), v((3, CUT, LANES), BF16), v((3, REST, LANES), BF16), v((3, CUT, LANES), BF16),
        v((3, REST, LANES), BF16), v((SIDE, SIDE, STACK, LANES), BF16),
        dma((8, 3)), dma((8, 3)), dma((3, SIDE)), dma((3, SIDE)), dma((2, 3, 3)), dma((2, 3, 3)),
        v((uses, TEAM - 1, INST, PIECE), BF16), v((uses, TEAM - 1, INST, PIECE), BF16),
        v((uses, INST, PIECE), BF16), v((uses, INST, PIECE), BF16),
        v((2, TEAM, INST, PIECE), BF16), v((TEAM, INST, PIECE), F32),
        dma((uses, TEAM - 1)), dma((uses, TEAM - 1)), dma((uses,)), dma((uses,)),
        dma((2, TEAM - 1)), dma((2, TEAM - 1)), dma((TEAM - 1,)), dma((TEAM - 1,)),
        v((rows, TEAM, 8, LANES), F32), v((2, 8, LANES), F32), v((2, 8, LANES), F32), v((SIDE, 8, LANES), F32),
        v((SIDE, 8, LANES), F32),
        dma((rows, TEAM - 1)), dma((rows, TEAM - 1)), dma((2,)), dma((2,)), dma((3,)), dma((3,)), dma((3,)), dma((3,)),
        v((INST, PIECE), F32), v((INST, PIECE), F32), v((INST, PIECE), F32), pltpu.SemaphoreType.REGULAR,
    ]
    outs = (
        jax.ShapeDtypeStruct((INST, COLS), F32),
        jax.ShapeDtypeStruct((INST, ROWS), F32),
        jax.ShapeDtypeStruct((INST, COLS), F32),
    )
    results = pl.pallas_call(
        kernel,
        out_shape=(v((INST, COLS), F32), v((INST, ROWS), F32), v((INST, COLS), F32)),
        in_specs=[anywhere] * 8,
        out_specs=(whole,) * 3,
        scratch_shapes=scratch,
        compiler_params=pltpu.CompilerParams(
            collective_id=0, has_side_effects=True, vmem_limit_bytes=58 * 2**20
        ),
        cost_estimate=pl.CostEstimate(flops=10**11, bytes_accessed=0, transcendentals=0),
    )(
        matrix,
        cost_pred,
        cost_true,
        dual_start,
        right_side.reshape(1, ROWS),
        bound_code.reshape(1, COLS),
        step_numer.T,
        step_denom.T,
    )
    return pl.pallas_call(
        keep,
        out_shape=outs,
        in_specs=[whole] * 3,
        out_specs=(anywhere,) * 3,
        scratch_shapes=[dma((9,))],
        compiler_params=pltpu.CompilerParams(vmem_limit_bytes=16 * 2**20),
    )(*results)


def solution(mesh):
    placed = (
        P("rows", "cols"),
        P(None, "cols"),
        P(None, "cols"),
        P(None, "rows"),
        P("rows"),
        P("cols"),
        P(),
        P(),
    )
    return jax.shard_map(
        local,
        mesh=mesh,
        in_specs=placed,
        out_specs=(P(None, "cols"), P(None, "rows"), P(None, "cols")),
        check_vma=False,
    )
```

```python
import jax
import jax.numpy as jnp
from jax import lax
from jax.experimental import pallas as pl
from jax.experimental.pallas import tpu as pltpu
from jax.sharding import PartitionSpec as P

VARS = 65536
MESH = pl.DeviceIdType.MESH
F32 = jnp.float32
BF16 = jnp.bfloat16
SHARP = 16.0
EPS = 1e-06

INST = 64
CUT = 80
ROWS = 1024
COLS = 4096
SIDE = 4
WIDE = COLS // SIDE
CHUNK = WIDE // SIDE
TEAM = 8
PIECE = ROWS // TEAM
LANES = 128
CUT_OUT = 80
STACK = INST * CHUNK // LANES
REST = STACK - CUT


def kernel(
    m_hbm, cp_hbm, ct_hbm, d0_hbm, right_hbm, code_hbm, numer_hbm, denom_hbm,
    primal_ref, dual_ref, grad_ref,
    m_ref, m_sem, cp_ref, ct_ref, d0_ref, right_ref, code_ref, numer_ref, denom_ref, in_sem,
    tau_ref, sigma_ref, theta_ref, scale2_ref, low_ref, high_ref, sum_ref,
    dbf_ref, own_ref, t0_ref, t1_ref, red0_ref, sh0_ref, slope0_ref, sa1_ref, e_ref, z_ref,
    s1x, s1z, r1x, r1z, s2z, s2x, r2z, r2x, gather,
    a_ss, a_rs, s_ss, s_rs, f_ss, f_rs,
    sb, rb, zs, zr, gb, gd,
    b_ss, b_rs, z_ss, z_rs, g_ss, g_rs, gd_ss, gd_rs,
    rows_t, rows_p, rows_pr, rowx, rowz,
    t_ss, t_rs, p_ss, p_rs, rx_ss, rx_rs, rz_ss, rz_rs,
    dual1_ref, weigh_ref, wimg_ref, far_in,
):
    rr = lax.axis_index("rows")
    cc = lax.axis_index("cols")
    x, zl = rr // SIDE, lax.rem(rr, SIDE)
    zh, yc = cc // TEAM, lax.rem(cc, TEAM)
    y = yc // 2

    def flip(value, k):
        if k == 0:
            return value
        total = value
        for bit in (1, 2, 4):
            if k & bit:
                total = total + bit - 2 * bit * lax.rem(value // bit, 2)
        return total

    def x_peer(k):
        return (flip(x, k) * SIDE + zl, cc)

    def z_peer(k):
        return (x * SIDE + flip(zl, k), cc)

    def team_peer(k):
        return (rr, zh * TEAM + flip(yc, k))

    far_peer = (rr, (1 - zh) * TEAM + yc)

    def remote(src, dst, send, recv, peer):
        copy = pltpu.make_async_remote_copy(
            src_ref=src, dst_ref=dst, send_sem=send, recv_sem=recv, device_id=peer, device_id_type=MESH
        )
        copy.start()
        return copy

    def at(value, size):
        return pl.ds(pl.multiple_of(value * size, size), size)

    order = (2, 1, 3, 0)
    near_last = (2, 3, 1)
    far_pieces = ((1, 1), (3, 1), (1, 3), (3, 3), (2, 1), (1, 2), (2, 3), (3, 2), (2, 2))
    team_order = (4, 5, 6, 7, 2, 3, 1)

    def load(n, src, dst):
        copy = pltpu.make_async_copy(src, dst, in_sem.at[n])
        copy.start()
        return copy

    load_d0 = load(0, d0_hbm, d0_ref)
    load_cp = load(1, cp_hbm, cp_ref)
    m_loads = []
    for k in order:
        cols = at(flip(x, k), WIDE)
        copy = pltpu.make_async_copy(m_hbm.at[:, cols], m_ref.at[:, cols], m_sem.at[k])
        copy.start()
        m_loads.append(copy)
    small_loads = [
        load(2, right_hbm, right_ref), load(3, code_hbm, code_ref),
        load(4, numer_hbm, numer_ref), load(5, denom_hbm, denom_ref),
    ]
    load_ct = load(6, ct_hbm, ct_ref)

    barrier = pltpu.get_barrier_semaphore()
    for k in (1, 2, 3):
        pl.semaphore_signal(barrier, inc=1, device_id=x_peer(k), device_id_type=MESH)
        pl.semaphore_signal(barrier, inc=1, device_id=z_peer(k), device_id_type=MESH)
    for k in range(1, TEAM):
        pl.semaphore_signal(barrier, inc=1, device_id=team_peer(k), device_id_type=MESH)

    border = 1 - lax.rem((zl + 1) // 2, 2)
    across = (x * SIDE + (SIDE - 1 - zl), (1 - zh) * TEAM + yc)

    @pl.when(border == 1)
    def _():
        pl.semaphore_signal(barrier, inc=1, device_id=across, device_id_type=MESH)


    lane = lax.broadcasted_iota(jnp.int32, (INST, LANES), 1)
    diagonal = lane == lax.broadcasted_iota(jnp.int32, (INST, LANES), 0)

    def to_row(column):
        spread = jnp.where(diagonal, jnp.broadcast_to(column, (INST, LANES)), 0.0)
        return jnp.broadcast_to(jnp.sum(spread, axis=0, keepdims=True), (8, LANES))

    def to_column(row):
        spread = jnp.where(diagonal, jnp.broadcast_to(row[0:1, :], (INST, LANES)), 0.0)
        return jnp.sum(spread, axis=1, keepdims=True)

    square = lax.broadcasted_iota(jnp.int32, (INST, INST), 1) == lax.broadcasted_iota(jnp.int32, (INST, INST), 0)

    def ratio(n):
        row = numer_ref[n : n + 1, :].astype(F32) / denom_ref[n : n + 1, :].astype(F32)
        return jnp.sum(jnp.where(square, jnp.broadcast_to(row, (INST, INST)), 0.0), axis=1, keepdims=True)

    def spread(column):
        return jnp.broadcast_to(column, (INST, LANES))

    def wait_all(copies):
        for c in copies:
            c.wait()

    def team_rows(which):
        return [
            remote(rows_t.at[which, yc], rows_t.at[which, yc], t_ss.at[which, k - 1], t_rs.at[which, k - 1], team_peer(k))
            for k in team_order
        ]

    def sum_team(which):
        total = rows_t[which, 0]
        for i in range(1, TEAM):
            total = total + rows_t[which, i]
        return total

    def far_row(which):
        return remote(rows_p.at[which], rows_pr.at[which], p_ss.at[which], p_rs.at[which], far_peer)

    def product(k):
        j = flip(x, k)
        out = jnp.dot(dbf_ref[...], m_ref[:, at(j, WIDE)], preferred_element_type=F32)
        for gz in range(SIDE):
            for part in range(CHUNK // LANES):
                start = gz * CHUNK + part * LANES
                own_ref[j, gz, part * INST : (part + 1) * INST] = out[:, start : start + LANES]
        if k:
            s1x[k - 1] = own_ref[j, :, :CUT].astype(BF16)
        for q in near_last:
            s1z[q - 1, j] = own_ref[j, flip(zl, q), CUT:].astype(BF16)

    def send_product(k):
        j = flip(x, k)
        sent_x = None
        if k:
            sent_x = remote(s1x.at[k - 1], r1x.at[k - 1], a_ss.at[0, k - 1], a_rs.at[0, k - 1], x_peer(k))
        sent_z = [
            remote(s1z.at[q - 1, j], r1z.at[q - 1, j], s_ss.at[q - 1, k], s_rs.at[q - 1, k], z_peer(q)) for q in near_last
        ]
        return sent_x, sent_z

    def scatter_dual():
        sends = {}
        for k in order:
            product(k)
            sends[k] = send_product(k)
        return sends

    def second_dual(sends):
        later = []

        def finish_z(k):
            j = flip(x, k)
            wait_all(sends[k][1])
            total = own_ref[j, zl, CUT:]
            for q in range(3):
                total = total + r1z[q, j].astype(F32)
            if k:
                s2x[k - 1] = total.astype(BF16)
                later.append(remote(s2x.at[k - 1], r2x.at[k - 1], a_ss.at[3, k - 1], a_rs.at[3, k - 1], x_peer(k)))
            else:
                t1_ref[...] = total

        finish_z(2)
        finish_z(1)
        for k in (1, 2, 3):
            sends[k][0].wait()
        t0_ref[...] = own_ref[x, :, :CUT] + r1x[0].astype(F32) + r1x[1].astype(F32) + r1x[2].astype(F32)
        for k in near_last:
            s2z[k - 1] = t0_ref[flip(zl, k)].astype(BF16)
            later.append(remote(s2z.at[k - 1], r2z.at[k - 1], a_ss.at[2, k - 1], a_rs.at[2, k - 1], z_peer(k)))
        finish_z(3)
        finish_z(0)
        return later

    def gather_dual(later, process, aside=None, before=None, process_far=None):
        wait_all(later)
        upper = t0_ref[zl] + r2z[0].astype(F32) + r2z[1].astype(F32) + r2z[2].astype(F32)
        lower = t1_ref[...] + r2x[0].astype(F32) + r2x[1].astype(F32) + r2x[2].astype(F32)
        gather[x, zl, :CUT] = upper.astype(BF16)
        gather[x, zl, CUT:] = lower.astype(BF16)
        above = pl.ds(0, CUT_OUT)
        below = pl.ds(CUT_OUT, STACK - CUT_OUT)
        mine_above = gather.at[x, zl, above]
        mine_below = gather.at[x, zl, below]
        z_own = {}
        x_own = {}
        z_more = {}
        x_more = {}
        for k in near_last:
            z_own[k] = remote(mine_above, mine_above, a_ss.at[4, k - 1], a_rs.at[4, k - 1], z_peer(k))
            x_own[k] = remote(mine_below, mine_below, a_ss.at[5, k - 1], a_rs.at[5, k - 1], x_peer(k))
        for k in near_last:
            z_more[k] = remote(mine_below, mine_below, a_ss.at[6, k - 1], a_rs.at[6, k - 1], z_peer(k))
            x_more[k] = remote(mine_above, mine_above, a_ss.at[7, k - 1], a_rs.at[7, k - 1], x_peer(k))
        if before is not None:
            before()
        process(x, zl)
        from_x = {}
        from_z = {}
        for k in (1, 3, 2):
            x_own[k].wait()
            part = gather.at[flip(x, k), zl, below]
            for q in near_last:
                from_z[k, q] = remote(part, part, f_ss.at[1, k - 1, q - 1], f_rs.at[1, k - 1, q - 1], z_peer(q))
            z_own[k].wait()
            part = gather.at[x, flip(zl, k), above]
            for q in near_last:
                from_x[q, k] = remote(part, part, f_ss.at[0, k - 1, q - 1], f_rs.at[0, k - 1, q - 1], x_peer(q))
        for k in (1, 3, 2):
            z_more[k].wait()
            process(x, flip(zl, k))
            x_more[k].wait()
            process(flip(x, k), zl)
        if aside is not None:
            aside()
        for qx, qz in far_pieces:
            from_x[qx, qz].wait()
            from_z[qx, qz].wait()
            (process_far or process)(flip(x, qx), flip(zl, qz))

    def halves(body):
        def process(gx, gz):
            for part in range(CHUNK // LANES):
                cols = at((gx * SIDE + gz) * (CHUNK // LANES) + part, LANES)
                image = gather[gx, gz, part * INST : (part + 1) * INST].astype(F32)
                body(image, cols)

        return process

    started = set()

    def with_product(body, rows, uses):
        done = halves(body)

        def process(gx, gz):
            done(gx, gz)
            cols = at(gx * SIDE + gz, CHUNK)
            out = lax.dot_general(
                e_ref[rows, cols], m_ref[:, cols], (((1,), (1,)), ((), ())), preferred_element_type=F32
            )
            for n, u in enumerate(uses):
                for i in range(TEAM):
                    part = out[n * INST : (n + 1) * INST, i * PIECE : (i + 1) * PIECE]
                    if u in started:
                        z_ref[u, i] += part
                    else:
                        z_ref[u, i] = part
            started.update(uses)

        return process

    def wide_image(u):
        for i in range(SIDE):
            out = lax.dot_general(
                e_ref[INST:, :], m_ref[i * 2 * PIECE : (i + 1) * 2 * PIECE, :], (((1,), (1,)), ((), ())),
                preferred_element_type=F32,
            )
            z_ref[u, 2 * i] = out[:, :PIECE]
            z_ref[u, 2 * i + 1] = out[:, PIECE:]

    def scatter_primal(u):
        sends = []
        for k in team_order:
            sb[u, k - 1] = z_ref[u, flip(yc, k)].astype(BF16)
            sends.append(remote(sb.at[u, k - 1], rb.at[u, k - 1], b_ss.at[u, k - 1], b_rs.at[u, k - 1], team_peer(k)))
        return sends

    def far_primal(u, sends):
        wait_all(sends)
        total = z_ref[u, yc]
        for k in range(1, TEAM):
            total = total + rb[u, k - 1].astype(F32)
        zs[u] = total.astype(BF16)
        return remote(zs.at[u], zr.at[u], z_ss.at[u], z_rs.at[u], far_peer)

    def done_primal(u, copy):
        copy.wait()
        return zs[u].astype(F32) + zr[u].astype(F32)

    def gather_primal(v):
        return [
            remote(gb.at[v, yc], gb.at[v, yc], g_ss.at[v, k - 1], g_rs.at[v, k - 1], team_peer(k)) for k in team_order
        ]

    def fill_dual(v):
        for i in range(TEAM):
            dbf_ref[:, i * PIECE : (i + 1) * PIECE] = gb[v, i]

    own_cols = at(yc, PIECE)

    load_d0.wait()
    dbf_ref[...] = d0_ref[...].astype(BF16)
    load_cp.wait()
    sum_ref[...] = jnp.zeros_like(sum_ref)

    def square_step(i, _):
        c = cp_ref[:, at(i, LANES)].astype(F32)
        sum_ref[...] += c * c
        return 0

    lax.fori_loop(0, COLS // LANES, square_step, 0, unroll=4)
    rows_t[0, yc] = to_row(jnp.sum(sum_ref[...], axis=1, keepdims=True))
    for position, k in enumerate(order):
        m_loads[position].wait()
        product(k)
    pl.semaphore_wait(barrier, 13 + border)

    @pl.when(border == 1)
    def _():
        pl.semaphore_signal(far_in, inc=1, device_id=across, device_id_type=MESH)

    sends = {k: send_product(k) for k in order}
    norm_copies = team_rows(0)

    wait_all(small_loads)
    load_ct.wait()
    code = code_ref[...]
    half_code = code // 2
    low_ref[...] = -0.25 - 0.75 * (code - 2 * half_code).astype(F32)
    high_ref[...] = 0.25 + 0.75 * half_code.astype(F32)
    theta_ref[...] = spread(ratio(2))

    @pl.when(border == 1)
    def _():
        pl.semaphore_wait(far_in, 1)
        pl.semaphore_signal(far_in, inc=1, device_id=z_peer(1), device_id_type=MESH)

    wait_all(norm_copies)
    rows_p[0] = sum_team(0)
    later = second_dual(sends)

    @pl.when(border == 0)
    def _():
        pl.semaphore_wait(far_in, 1)

    norm_far = far_row(0)

    def steps_of_scale():
        norm_far.wait()
        norm_sum = to_column(rows_p[0] + rows_pr[0])
        scale = jnp.sqrt(norm_sum / VARS + EPS)
        tau_ref[...] = spread(ratio(0) / scale)
        sigma_ref[...] = spread(ratio(1) * scale)
        scale2_ref[...] = spread(VARS * scale * scale)

    def first_step(image, cols):
        reduced = cp_ref[:, cols].astype(F32) - image
        shifted = 0.0 - tau_ref[...] * reduced
        projected = jnp.minimum(jnp.maximum(shifted, low_ref[:, cols]), high_ref[:, cols])
        red0_ref[:, cols] = reduced
        sh0_ref[:, cols] = shifted
        e_ref[:INST, cols] = (projected + theta_ref[...] * projected).astype(BF16)

    gather_dual(later, with_product(first_step, slice(0, INST), (0,)), before=steps_of_scale)

    sends = scatter_primal(0)

    def slope_of(shifted, cols):
        return jax.nn.sigmoid(SHARP * (shifted - low_ref[:, cols])) * jax.nn.sigmoid(
            SHARP * (high_ref[:, cols] - shifted)
        )

    far = far_primal(0, sends)
    image = done_primal(0, far)
    residue0 = right_ref[:, own_cols] - image
    dual1 = d0_ref[:, own_cols] + sigma_ref[...] * residue0
    gb[0, yc] = dual1.astype(BF16)
    gathers = gather_primal(0)
    dual1_ref[...] = dual1
    weigh_ref[...] = sigma_ref[...] * residue0
    wait_all(gathers)
    fill_dual(0)

    sends = scatter_dual()
    def slope_step(i, _):
        cols = at(i, LANES)
        slope = slope_of(sh0_ref[:, cols], cols)
        slope0_ref[:, cols] = slope
        e_ref[INST:, cols] = (slope * red0_ref[:, cols]).astype(BF16)
        return 0

    lax.fori_loop(0, COLS // LANES, slope_step, 0, unroll=2)
    wide_image(1)
    weigh_sends = scatter_primal(1)
    later = second_dual(sends)

    def second_step(image, cols):
        low, high = low_ref[:, cols], high_ref[:, cols]
        reduced = cp_ref[:, cols].astype(F32) - image
        before = jnp.minimum(jnp.maximum(sh0_ref[:, cols], low), high)
        shifted = before - tau_ref[...] * reduced
        primal_ref[:, cols] = shifted
        grad_ref[:, cols] = reduced
        slope_adj = slope_of(shifted, cols) * ct_ref[:, cols].astype(F32)
        sa1_ref[:, cols] = slope_adj
        e_ref[:INST, cols] = (tau_ref[...] * slope_adj).astype(BF16)

    def primal_step(image, cols):
        low, high = low_ref[:, cols], high_ref[:, cols]
        before = jnp.minimum(jnp.maximum(sh0_ref[:, cols], low), high)
        projected = jnp.minimum(jnp.maximum(primal_ref[:, cols], low), high)
        primal_ref[:, cols] = projected
        e_ref[INST:, cols] = (projected + theta_ref[...] * (projected - before)).astype(BF16)
        slope_adj = sa1_ref[:, cols]
        sum_ref[...] += slope_adj * grad_ref[:, cols] + slope_adj * (slope0_ref[:, cols] * red0_ref[:, cols])

    def both_steps(image, cols):
        second_step(image, cols)
        primal_step(image, cols)

    sum_ref[...] = jnp.zeros_like(sum_ref)
    gather_dual(
        later,
        with_product(both_steps, slice(0, 2 * INST), (2, 3)),
        process_far=with_product(second_step, slice(0, INST), (2,)),
    )

    sends = scatter_primal(2)
    weigh_far = far_primal(1, weigh_sends)
    primal_process = with_product(primal_step, slice(INST, 2 * INST), (3,))
    for qx, qz in far_pieces:
        primal_process(flip(x, qx), flip(zl, qz))
    rows_t[1, yc] = to_row(tau_ref[:, 0:1] * jnp.sum(sum_ref[...], axis=1, keepdims=True))
    far = far_primal(2, sends)
    end_sends = scatter_primal(3)
    factor_copies = team_rows(1)
    adjoint = done_primal(2, far)
    rounded = adjoint.astype(BF16)
    gb[1, yc] = rounded
    gathers = gather_primal(1)
    wimg_ref[...] = tau_ref[...] * (1.0 + theta_ref[...]) * sigma_ref[...] * done_primal(1, weigh_far)
    weighed = adjoint * weigh_ref[...] - rounded.astype(F32) * wimg_ref[...]
    rows_t[2, yc] = to_row(jnp.sum(weighed, axis=1, keepdims=True))
    wait_all(factor_copies)
    factor_copies = team_rows(2)
    rows_p[1] = sum_team(1)
    factor_far = far_row(1)
    wait_all(gathers)
    fill_dual(1)

    sends = scatter_dual()
    end_far = far_primal(3, end_sends)
    wait_all(factor_copies)
    rowx[x] = sum_team(2)
    x_rows = [remote(rowx.at[x], rowx.at[x], rx_ss.at[k - 1], rx_rs.at[k - 1], x_peer(k)) for k in (1, 2, 3)]
    later = second_dual(sends)
    wait_all(x_rows)
    rowz[zl] = rowx[0] + rowx[1] + rowx[2] + rowx[3]
    z_rows = [remote(rowz.at[zl], rowz.at[zl], rz_ss.at[k - 1], rz_rs.at[k - 1], z_peer(k)) for k in (1, 2, 3)]
    factor_far.wait()
    residue1 = right_ref[:, own_cols] - done_primal(3, end_far)
    gd[yc] = dual1_ref[...] + sigma_ref[...] * residue1
    dual_gathers = [
        remote(gd.at[yc], gd.at[yc], gd_ss.at[k - 1], gd_rs.at[k - 1], team_peer(k)) for k in team_order
    ]
    wait_all(z_rows)
    factors = to_column(rows_p[1] + rows_pr[1] + (rowz[0] + rowz[1] + rowz[2] + rowz[3]))
    sum_ref[...] = spread(factors) / scale2_ref[...]

    def last_step(image, cols):
        slope_adj = sa1_ref[:, cols]
        ahead = slope_adj - (1.0 + theta_ref[...]) * (sigma_ref[...] * image)
        gradient = tau_ref[...] * (slope_adj + slope0_ref[:, cols] * ahead)
        grad_ref[:, cols] = cp_ref[:, cols].astype(F32) * sum_ref[...] - gradient

    def dual_end():
        wait_all(dual_gathers)
        for i in range(TEAM):
            dual_ref[:, i * PIECE : (i + 1) * PIECE] = gd[i]

    gather_dual(later, halves(last_step), dual_end)


def keep(a, b, c, out_a, out_b, out_c, sem):
    ways = [(b, out_b)]
    for n in range(4):
        rows = pl.ds(n * 16, 16)
        ways.append((a.at[rows], out_a.at[rows]))
        ways.append((c.at[rows], out_c.at[rows]))
    stores = [pltpu.make_async_copy(src, dst, sem.at[n]) for n, (src, dst) in enumerate(ways)]
    for copy in stores:
        copy.start()
    for copy in stores:
        copy.wait()


def local(matrix, cost_pred, cost_true, dual_start, right_side, bound_code, step_numer, step_denom):
    dma = pltpu.SemaphoreType.DMA
    v = pltpu.VMEM
    anywhere = pl.BlockSpec(memory_space=pl.ANY)
    whole = pl.BlockSpec(memory_space=pltpu.VMEM)
    uses, rows = 4, 3
    scratch = [
        v((ROWS, COLS), BF16), dma((SIDE,)), v((INST, COLS), BF16), v((INST, COLS), BF16), v((INST, ROWS), F32),
        v((1, ROWS), F32), v((1, COLS), jnp.int32), v((3, INST), jnp.int32), v((3, INST), jnp.int32), dma((7,)),
        v((INST, LANES), F32), v((INST, LANES), F32), v((INST, LANES), F32), v((INST, LANES), F32),
        v((1, COLS), F32), v((1, COLS), F32), v((INST, LANES), F32),
        v((INST, ROWS), BF16), v((SIDE, SIDE, STACK, LANES), F32), v((SIDE, CUT, LANES), F32), v((REST, LANES), F32),
        v((INST, COLS), F32), v((INST, COLS), F32), v((INST, COLS), F32),
        v((INST, COLS), F32), v((2 * INST, COLS), BF16), v((uses, TEAM, INST, PIECE), F32),
        v((3, SIDE, CUT, LANES), BF16), v((3, SIDE, REST, LANES), BF16), v((3, SIDE, CUT, LANES), BF16),
        v((3, SIDE, REST, LANES), BF16), v((3, CUT, LANES), BF16), v((3, REST, LANES), BF16), v((3, CUT, LANES), BF16),
        v((3, REST, LANES), BF16), v((SIDE, SIDE, STACK, LANES), BF16),
        dma((8, 3)), dma((8, 3)), dma((3, SIDE)), dma((3, SIDE)), dma((2, 3, 3)), dma((2, 3, 3)),
        v((uses, TEAM - 1, INST, PIECE), BF16), v((uses, TEAM - 1, INST, PIECE), BF16),
        v((uses, INST, PIECE), BF16), v((uses, INST, PIECE), BF16),
        v((2, TEAM, INST, PIECE), BF16), v((TEAM, INST, PIECE), F32),
        dma((uses, TEAM - 1)), dma((uses, TEAM - 1)), dma((uses,)), dma((uses,)),
        dma((2, TEAM - 1)), dma((2, TEAM - 1)), dma((TEAM - 1,)), dma((TEAM - 1,)),
        v((rows, TEAM, 8, LANES), F32), v((2, 8, LANES), F32), v((2, 8, LANES), F32), v((SIDE, 8, LANES), F32),
        v((SIDE, 8, LANES), F32),
        dma((rows, TEAM - 1)), dma((rows, TEAM - 1)), dma((2,)), dma((2,)), dma((3,)), dma((3,)), dma((3,)), dma((3,)),
        v((INST, PIECE), F32), v((INST, PIECE), F32), v((INST, PIECE), F32), pltpu.SemaphoreType.REGULAR,
    ]
    outs = (
        jax.ShapeDtypeStruct((INST, COLS), F32),
        jax.ShapeDtypeStruct((INST, ROWS), F32),
        jax.ShapeDtypeStruct((INST, COLS), F32),
    )
    results = pl.pallas_call(
        kernel,
        out_shape=(v((INST, COLS), F32), v((INST, ROWS), F32), v((INST, COLS), F32)),
        in_specs=[anywhere] * 8,
        out_specs=(whole,) * 3,
        scratch_shapes=scratch,
        compiler_params=pltpu.CompilerParams(
            collective_id=0, has_side_effects=True, vmem_limit_bytes=58 * 2**20
        ),
        cost_estimate=pl.CostEstimate(flops=10**11, bytes_accessed=0, transcendentals=0),
    )(
        matrix,
        cost_pred,
        cost_true,
        dual_start,
        right_side.reshape(1, ROWS),
        bound_code.reshape(1, COLS),
        step_numer.T,
        step_denom.T,
    )
    return pl.pallas_call(
        keep,
        out_shape=outs,
        in_specs=[whole] * 3,
        out_specs=(anywhere,) * 3,
        scratch_shapes=[dma((9,))],
        compiler_params=pltpu.CompilerParams(vmem_limit_bytes=16 * 2**20),
    )(*results)


def solution(mesh):
    placed = (
        P("rows", "cols"),
        P(None, "cols"),
        P(None, "cols"),
        P(None, "rows"),
        P("rows"),
        P("cols"),
        P(),
        P(),
    )
    return jax.shard_map(
        local,
        mesh=mesh,
        in_specs=placed,
        out_specs=(P(None, "cols"), P(None, "rows"), P(None, "cols")),
        check_vma=False,
    )
```
